32 devices in a mesh: group: 2 (over y), dev: 16 (over z, x, core).
Axes of the slice: x: 2, y: 2, z: 4, core: 2. Of those that a mesh axis runs over, the one named last changes fastest.
Arguments:
- source_emb: float32 [256, 128, 128], P(('group', 'dev')), may hold values from -6 to 6
- target_emb: float32 [1024, 128, 128], P(('group', 'dev')), may hold values from -6 to 6
- source_mass: float32 [256, 128], P(('group', 'dev')), may hold values from 0.5 to 2
- target_mass: float32 [1024, 128], P(('group', 'dev')), may hold values from 0.5 to 2
- cand_device: int32 [256, 7], P(('group', 'dev')), may hold values from 0 to 15, all different within a row; in each aligned block of 8 rows (0 to 7, 8 to 15, ...) at most 5 rows name the same one
- cand_block: int32 [256, 8], P(('group', 'dev')), may hold values from 0 to 31
Outputs:
- src_scale: float32 [256, 128], P(('group', 'dev'))
- tgt_scale: float32 [1024, 128], P(('group', 'dev'))
The draws below stay inside these ranges and needn't reach their ends.
Inputs may be any that keep to these rules, and one draw needn't show every extreme that they name: `cand_device`: the seven devices named by one source block are distinct; among the 8 source blocks of one device, no device is named more than 5 times, and some device is named exactly 5 times.
All inputs are finite; a program needn't handle non-finite values.
Results may differ from the reference program's by a relative error of at most 0.0001.
Values sent between devices are 32-bit elements; how exact they have to be, the bound alone decides.
No kernel may reach another device: no remote copies, remote signals or barrier semaphores. Data moves between devices by JAX's collectives and lax.ppermute only.
A program may use at most 64 MiB of HBM per device.

```python
import math
import jax
import jax.numpy as jnp
import numpy as np
from jax import lax

SB_DEV = 8
TB_DEV = 32
NODE_GROUP_SIZE = 128
FEATURE_LENGTH = 128
ITERS = 2
CAP = 5
NSB = 256
NTB = 1024
N_GROUP = 2
N_DEV = 16


def touch_ends(result, own_key, least, high):
    longest = result.shape.index(max(result.shape))
    spots = []
    for shift in (0, 1):
        where = [jax.random.randint(jax.random.fold_in(own_key, axis), (), 0, length) for axis, length in enumerate(result.shape)]
        where[longest] = (where[longest] + shift) % result.shape[longest]
        spots.append(tuple(where))
    return result.at[spots[0]].set(least).at[spots[1]].set(high)


def block_levels(key, dims, split, least, top_value):
    def one(axis_at, shards_of):
        draws = jax.random.uniform(jax.random.fold_in(jax.random.fold_in(key, 6), axis_at), (shards_of,), jnp.float32, least / len(split), top_value / len(split))
        return jnp.repeat(jnp.exp(draws), dims[axis_at] // shards_of).reshape((-1,) + (1,) * (len(dims) - axis_at - 1))

    gain = one(*split[0])
    for cut in split[1:]:
        gain = gain * one(*cut)
    return gain


def shared_out(key, own, number, rows, count, top, reach, skew):
    sequence = jax.random.permutation(key, count)
    crowded, common = shares(count, rows * top, reach, skew, True), shares(count, rows * top, reach, skew, False)
    places = jnp.arange(count)

    def named(tallies, rotation):
        used = int((tallies > 0).sum())
        fixed = max(1, used // 4)
        moved = fixed + (places - fixed + rotation * (used - fixed)) % max(1, count - fixed)
        return jnp.zeros((count,), jnp.int32).at[sequence[jnp.where(places < fixed, places, moved)]].set(jnp.asarray(tallies, jnp.int32))

    tallies = jnp.where(number % 4 == 0, named(crowded, number // 4), named(common, number - number // 4 - 1))
    mixed = jax.random.permutation(jax.random.fold_in(own, 3), count)
    giver, receiver = mixed[0:count // 2 * 2:2], mixed[1:count // 2 * 2:2]
    slack = jnp.minimum(tallies[giver] - 1, reach - tallies[receiver]) // 2
    slack = jnp.where((giver == sequence[0]) | (receiver == sequence[0]) | (tallies[receiver] == 0), 0, jnp.maximum(slack, 0))
    moved = jax.random.randint(jax.random.fold_in(own, 4), (count // 2,), 0, 1 << 20) % (slack + 1)
    tallies = tallies.at[giver].add(-moved).at[receiver].add(moved)
    labels = jnp.searchsorted(jnp.cumsum(tallies), jnp.arange(rows * top), side="right").astype(jnp.int32)
    listing = labels.reshape(top, rows).T
    listing = listing[jax.random.permutation(jax.random.fold_in(own, 1), rows)]
    rotation = jax.random.randint(jax.random.fold_in(own, 2), (rows, 1), 0, top)
    return jnp.take_along_axis(listing, (jnp.arange(top)[None, :] + rotation) % top, axis=1)


def shares(number_of, total, reach, lean, full):
    weights = [(1 << 20) // math.isqrt(standing ** lean) + 1 for standing in range(1, number_of + 1)]
    largest = reach if full else min(reach, max(-(-total // number_of), total * weights[0] // sum(weights)))
    least = 1 if total - largest >= number_of - 1 else 0
    holding, surplus = [largest] + [least] * (number_of - 1), total - largest - least * (number_of - 1)
    while surplus > 0:
        free = [i for i in range(1, number_of) if holding[i] < largest] or [i for i in range(1, number_of) if holding[i] < reach]
        pool, remaining = sum([weights[i] for i in free]), surplus
        for i in free:
            extra = min(reach - holding[i], max(1, remaining * weights[i] // pool), surplus)
            holding[i] = holding[i] + extra
            surplus = surplus - extra
    return np.array(holding)


def gaussian(key, extent, deviation, bound, cuts=(), kind=jnp.bfloat16):
    level = block_levels(key, extent, cuts, -0.22, 0.18) if cuts else 1.0
    result = jax.random.normal(key, extent, jnp.float32) * deviation * level
    return jnp.minimum(jnp.maximum(result, -bound), bound).astype(kind)


def setup_inputs(seed: int = 0) -> dict:
    splits = jax.random.split(jax.random.key(seed), 7)
    source_emb = gaussian(splits[0], (NSB, NODE_GROUP_SIZE, FEATURE_LENGTH), 1.0, 6.0, ((0, 32),), jnp.float32)
    target_emb = gaussian(splits[1], (NTB, NODE_GROUP_SIZE, FEATURE_LENGTH), 1.0, 6.0, ((0, 32),), jnp.float32)
    source_mass = jnp.clip(jnp.exp(math.log(2.0) - 1.3862944 * jax.random.uniform(splits[2], (NSB, NODE_GROUP_SIZE), jnp.float32) ** block_levels(splits[2], (NSB, NODE_GROUP_SIZE), ((0, 32),), -0.2, 0.2)), 0.5, 2.0)
    target_mass = jnp.clip(jnp.exp(math.log(2.0) - 1.3862944 * jax.random.uniform(splits[3], (NTB, NODE_GROUP_SIZE), jnp.float32) ** block_levels(splits[3], (NTB, NODE_GROUP_SIZE), ((0, 32),), -0.2, 0.2)), 0.5, 2.0)
    cand_device_keys = jax.random.split(jax.random.fold_in(splits[4], 1), NSB // SB_DEV)
    cand_device_turns = jax.random.permutation(jax.random.fold_in(splits[4], 3), NSB // SB_DEV)
    cand_device = jax.vmap(lambda own, number: shared_out(jax.random.fold_in(splits[4], 2), own, number, SB_DEV, N_DEV, 7, CAP, 2))(cand_device_keys, cand_device_turns).reshape((NSB, 7))
    cand_block = touch_ends(jax.random.randint(splits[5], (NSB, 8), 0, TB_DEV), jax.random.fold_in(splits[5], 1), 0, TB_DEV - 1).astype(jnp.int32)
    return {"source_emb": source_emb, "target_emb": target_emb, "source_mass": source_mass, "target_mass": target_mass, "cand_device": cand_device, "cand_block": cand_block}


entropic_regularizer = 0.1
dustbin = 0.5
epsilon = 1e-06

def unit_rows(emb):
    return emb * lax.rsqrt(lax.optimization_barrier(jnp.mean(emb * emb, axis=-1, keepdims=True)) + epsilon)

def target_ids(cand_device, cand_block):
    src_index = jnp.arange(cand_device.shape[0], dtype=jnp.int32)
    flat_dev = src_index // SB_DEV
    cluster_label = flat_dev // N_DEV
    dev_index = flat_dev % N_DEV
    near_ids = (cluster_label[:, None] * N_DEV + cand_device) * TB_DEV + cand_block[:, :7]
    far_ids = ((cluster_label + 1) % N_GROUP * N_DEV + dev_index) * TB_DEV + cand_block[:, 7]
    return jnp.concatenate([near_ids, far_ids[:, None]], axis=1).astype(jnp.int32)

def kernel_tile(left_node_group, tgt_blocks):
    alignment_affinity = jnp.einsum('bd,kjd->kbj', left_node_group, tgt_blocks, precision=lax.Precision.HIGHEST)
    return jnp.exp(alignment_affinity * (1.0 / (FEATURE_LENGTH * entropic_regularizer))) / (8.0 * NODE_GROUP_SIZE)

def reference(source_emb, target_emb, source_mass, target_mass, cand_device, cand_block):
    src_unit = unit_rows(source_emb)
    tgt_unit = unit_rows(target_emb)
    cand_ids = target_ids(cand_device, cand_block)
    tgt_scale = jnp.ones_like(target_mass)
    src_scale = jnp.ones_like(source_mass)
    for sweep in range(ITERS):

        def rows_of(packed, tgt_scale=tgt_scale):
            left_node_group, id_block = packed
            kernel = kernel_tile(left_node_group, tgt_unit[id_block])
            return jnp.einsum('kbj,kj->b', kernel, tgt_scale[id_block], precision=lax.Precision.HIGHEST)
        row_sums = lax.map(rows_of, (src_unit, cand_ids))
        src_scale = source_mass / (dustbin + row_sums)

        def cols_of(packed):
            left_node_group, id_block, scale_block = packed
            kernel = kernel_tile(left_node_group, tgt_unit[id_block])
            return jnp.einsum('kbj,b->kj', kernel, scale_block, precision=lax.Precision.HIGHEST)
        col_parts = lax.map(cols_of, (src_unit, cand_ids, src_scale))
        col_sums = jax.ops.segment_sum(col_parts.reshape(-1, NODE_GROUP_SIZE), cand_ids.reshape(-1), num_segments=NTB)
        tgt_scale = target_mass / (dustbin + col_sums)
    return (src_scale, tgt_scale)
```

```python
import functools

import jax
import jax.numpy as jnp
from jax import lax
from jax.experimental import pallas as pl
from jax.experimental.pallas import tpu as pltpu
from jax.sharding import PartitionSpec as P

ITERS = 2

entropic_regularizer = 0.1
dustbin = 0.5
epsilon = 1e-06

VMEM = pl.BlockSpec(memory_space=pltpu.VMEM)
SMEM = pl.BlockSpec(memory_space=pltpu.SMEM)
NT = (((1,), (1,)), ((), ()))
NN = (((1,), (0,)), ((), ()))


def split2(x):
    high = x.astype(jnp.bfloat16)
    low = (x - high.astype(jnp.float32)).astype(jnp.bfloat16)
    return high, low


def unit(x):
    return x * lax.rsqrt(jnp.mean(x * x, axis=-1, keepdims=True) + epsilon)


def stacked_parts(row):
    x = jnp.broadcast_to(row, (8, row.shape[1]))
    high = x.astype(jnp.bfloat16).astype(jnp.float32)
    rest = x - high
    low = rest.astype(jnp.bfloat16).astype(jnp.float32)
    place = lax.broadcasted_iota(jnp.int32, x.shape, 0)
    parts = jnp.where(place == 0, high, jnp.where(place == 1, low, jnp.where(place == 2, rest - low, 0.0)))
    return parts.astype(jnp.bfloat16)


def column_product(parts, tile):
    both = lax.dot_general(parts, tile, NN, preferred_element_type=jnp.float32)
    width = tile.shape[1] // 2
    return both[:, :width] + both[:, width:]


def row_product(parts, tile):
    return lax.dot_general(
        jnp.concatenate([parts, parts], axis=1), tile, NT, preferred_element_type=jnp.float32
    )


def target_kernel(emb_ref, out_ref):
    def one(block, carry):
        high, low = split2(unit(emb_ref[block]).T)
        out_ref[block] = jnp.concatenate([high, low], axis=1)
        return carry

    lax.fori_loop(0, emb_ref.shape[0], one, 0, unroll=2)


def target_operand(emb):
    blocks, rows, width = emb.shape
    return pl.pallas_call(
        target_kernel,
        out_shape=jax.ShapeDtypeStruct((blocks, width, 2 * rows), jnp.bfloat16),
        in_specs=[VMEM],
        out_specs=VMEM,
        cost_estimate=pl.CostEstimate(flops=0, bytes_accessed=3 * emb.size * 4, transcendentals=0),
        compiler_params=pltpu.CompilerParams(vmem_limit_bytes=32 << 20),
        name="target_operand",
    )(emb)


def tile_kernel(chunks, sides, slots, sb, half, *refs):
    loc, tgt = refs[:2]
    source = refs[2 : 2 + 2 * chunks]
    weight = refs[2 + 2 * chunks : 2 + 2 * chunks + sides]
    tiles, sums, partial = refs[2 + 2 * chunks + sides :]
    width = source[0].shape[1]
    scale = 1.0 / (width * entropic_regularizer)
    partial[...] = jnp.zeros_like(partial)
    place = lax.broadcasted_iota(jnp.int32, (8, 2 * width), 0)
    ones = jnp.where(place == 0, 1.0, 0.0).astype(jnp.bfloat16)
    for chunk in range(chunks):
        upper, lower = source[2 * chunk], source[2 * chunk + 1]
        for side in range(sides):
            for j in range(slots):
                at = (chunk * sides + side) * slots + j
                block = loc[at]
                start = pl.multiple_of(lax.rem(block, sb) * half, half)
                left = jnp.concatenate([upper[pl.ds(start, half)], lower[pl.ds(start, half)]], axis=0)
                high, low = split2(unit(left))
                right = weight[side][tgt[at]]
                both = lax.dot_general(
                    jnp.concatenate([high, low], axis=1),
                    jnp.concatenate([right, right], axis=0),
                    NN,
                    preferred_element_type=jnp.float32,
                )
                nodes = both.shape[1] // 2
                affinity = both[:, :nodes] + both[:, nodes:]
                tile = jnp.exp(affinity * scale) * (1.0 / (8.0 * nodes))
                tile = jnp.concatenate(split2(tile), axis=1)
                tiles[at] = tile
                spot = chunk * (sb + 1) + block
                partial[spot] += lax.dot_general(ones, tile, NT, preferred_element_type=jnp.float32)
        for block in range(sb):
            sums[chunk, block : block + 1] = partial[chunk * (sb + 1) + block][0:1]


def build_tiles(source, weight, loc, tgt, slots, sb):
    chunks, sides = len(source) // 2, len(weight)
    half, width = source[0].shape[0] // sb - 1, source[0].shape[1]
    nodes = weight[0].shape[2] // 2
    count = chunks * sides * slots
    return pl.pallas_call(
        functools.partial(tile_kernel, chunks, sides, slots, sb, half),
        out_shape=(
            jax.ShapeDtypeStruct((count, 2 * half, 2 * nodes), jnp.bfloat16),
            jax.ShapeDtypeStruct((chunks, sb, 2 * half), jnp.float32),
        ),
        in_specs=[SMEM, SMEM] + [VMEM] * (len(source) + sides),
        out_specs=(VMEM, VMEM),
        scratch_shapes=[pltpu.VMEM((chunks * (sb + 1), 8, 2 * half), jnp.float32)],
        cost_estimate=pl.CostEstimate(
            flops=count * 2 * half * nodes * width * 8,
            bytes_accessed=count * 2 * half * nodes * 4 + sides * weight[0].size * 2,
            transcendentals=count * 2 * half * nodes,
        ),
        compiler_params=pltpu.CompilerParams(vmem_limit_bytes=40 << 20),
        name="build_tiles",
    )(loc, tgt, *source, *weight)


def column_kernel(near, far, rows_at, sums_at, far_at, rows, mass, far_rows, far_mass, *refs):
    tiles, out, scale, total = refs[: len(near) + 1], refs[-3], refs[-2], refs[-1]
    count = rows.shape[0]
    scale[...] = jnp.zeros_like(scale)
    scale[0:count] = mass[...] / (dustbin + rows[...])
    scale[count + 8 : count + 8 + far] = far_mass[...] / (dustbin + far_rows[...])
    total[...] = jnp.zeros_like(total)
    base = 0
    for part, slots in enumerate(near):

        def one(slot, carry, part=part, base=base):
            at = base + slot
            parts = stacked_parts(scale[pl.ds(rows_at[at], 1), :])
            total[sums_at[at]] += column_product(parts, tiles[part][slot])
            return carry

        lax.fori_loop(0, slots, one, 0, unroll=True)
        base += slots
    for slot in range(far):
        parts = stacked_parts(scale[count + 8 + slot : count + 9 + slot, :])
        total[far_at[slot]] += column_product(parts, tiles[len(near)][slot])
    for block in range(out.shape[0]):
        out[block : block + 1] = jnp.sum(total[block], axis=0, keepdims=True)


def column_sums(tables, rows, mass, far_rows, far_mass, tiles, targets):
    near = tuple(t.shape[0] for t in tiles[:-1])
    far, nodes = tiles[-1].shape[0], tiles[-1].shape[2] // 2
    width = rows.shape[1]
    return pl.pallas_call(
        functools.partial(column_kernel, near, far),
        out_shape=jax.ShapeDtypeStruct((targets, nodes), jnp.float32),
        in_specs=[SMEM] * 3 + [VMEM] * (4 + len(tiles)),
        out_specs=VMEM,
        scratch_shapes=[
            pltpu.VMEM((rows.shape[0] + 8 + (far + 7) // 8 * 8, width), jnp.float32),
            pltpu.VMEM((targets + 1, 8, nodes), jnp.float32),
        ],
        cost_estimate=pl.CostEstimate(
            flops=sum(t.size for t in tiles) * 16, bytes_accessed=sum(t.size for t in tiles) * 2, transcendentals=0
        ),
        compiler_params=pltpu.CompilerParams(vmem_limit_bytes=40 << 20),
        name="column_sums",
    )(*tables, rows, mass, far_rows, far_mass, *tiles)


def row_kernel(near, far, rows_at, sums_at, far_at, mine, theirs, mass, other_mass, *refs):
    tiles, out, far_out, scale, total = refs[: len(near) + 1], refs[-4], refs[-3], refs[-2], refs[-1]
    blocks = mass.shape[0]
    scale[...] = jnp.zeros_like(scale)
    scale[0:blocks] = mass[...] / (dustbin + mine[0:blocks] + theirs[blocks : 2 * blocks])
    scale[blocks : 2 * blocks] = other_mass[...] / (dustbin + mine[blocks : 2 * blocks] + theirs[0:blocks])
    total[...] = jnp.zeros_like(total)
    base = 0
    for part, slots in enumerate(near):

        def one(slot, carry, part=part, base=base):
            at = base + slot
            parts = stacked_parts(scale[pl.ds(sums_at[at], 1), :])
            total[rows_at[at]] += row_product(parts, tiles[part][slot])
            return carry

        lax.fori_loop(0, slots, one, 0, unroll=True)
        base += slots
    for slot in range(far):
        parts = stacked_parts(scale[pl.ds(far_at[slot], 1), :])
        far_out[slot : slot + 1] = jnp.sum(row_product(parts, tiles[len(near)][slot]), axis=0, keepdims=True)
    for block in range(out.shape[0]):
        out[block : block + 1] = jnp.sum(total[block], axis=0, keepdims=True)


def row_sums(tables, mine, theirs, mass, other_mass, tiles, sources):
    near = tuple(t.shape[0] for t in tiles[:-1])
    far, nodes = tiles[-1].shape[0], tiles[-1].shape[2] // 2
    width = tiles[-1].shape[1]
    return pl.pallas_call(
        functools.partial(row_kernel, near, far),
        out_shape=(
            jax.ShapeDtypeStruct((sources, width), jnp.float32),
            jax.ShapeDtypeStruct((far, width), jnp.float32),
        ),
        in_specs=[SMEM] * 3 + [VMEM] * (4 + len(tiles)),
        out_specs=(VMEM, VMEM),
        scratch_shapes=[
            pltpu.VMEM((mine.shape[0] + 8, nodes), jnp.float32),
            pltpu.VMEM((sources + 1, 8, width), jnp.float32),
        ],
        cost_estimate=pl.CostEstimate(
            flops=sum(t.size for t in tiles) * 16, bytes_accessed=sum(t.size for t in tiles) * 2, transcendentals=0
        ),
        compiler_params=pltpu.CompilerParams(vmem_limit_bytes=40 << 20),
        name="row_sums",
    )(*tables, mine, theirs, mass, other_mass, *tiles)


def local(source_emb, target_emb, source_mass, target_mass, cand_device, cand_block):
    dev_count = lax.axis_size("dev")
    group_count = lax.axis_size("group")
    chips = dev_count // 2
    sb, rows, width = source_emb.shape
    tb = target_emb.shape[0]
    near_count = cand_device.shape[1]
    slot_cap = (near_count * sb + dev_count - 1) // dev_count + 1
    half = rows // 2

    ring = list(range(0, chips, 2)) + list(range(chips - 1, 0, -2))
    spot_of = [ring.index(chip) for chip in range(chips)]
    steps = chips // 2

    def around(x, by):
        pairs = [
            (2 * ring[i] + core, 2 * ring[(i + by) % chips] + core) for i in range(chips) for core in range(2)
        ]
        return lax.ppermute(x, "dev", pairs)

    def across(x, bit):
        return lax.ppermute(x, "dev", [(i, i ^ bit) for i in range(dev_count)])

    def along_group(x, by):
        return lax.ppermute(x, "group", [(i, (i + by) % group_count) for i in range(group_count)])

    device = lax.axis_index("dev")
    chip = device // 2
    spot = jnp.asarray(spot_of, jnp.int32)[chip]

    def chip_at(offset):
        return jnp.asarray(ring, jnp.int32)[(spot + offset + chips) % chips]

    candidates = jnp.concatenate([cand_device, cand_block], axis=1).astype(jnp.float32)
    candidates = jnp.pad(candidates, ((0, 0), (0, width - candidates.shape[1])))
    upper = jnp.concatenate([source_emb[:, :half].reshape(sb * half, width), candidates], axis=0)
    lower = jnp.concatenate([source_emb[:, half:].reshape(sb * half, width), source_mass], axis=0)

    sibling_emb = across(target_emb, 1)
    sibling_mass = across(target_mass, 1)

    own_weight = target_operand(target_emb)
    sibling_weight = target_operand(sibling_emb)
    weights = (own_weight, sibling_weight)

    sides = jnp.stack([device, device ^ 1])

    def tables_of(upper_chunk, chip_index):
        meta = upper_chunk[sb * half :].astype(jnp.int32)
        named, block = meta[:, :near_count], meta[:, near_count : 2 * near_count]
        hit = (named[None] == sides[:, None, None]).astype(jnp.int32)
        valid = jnp.sum(hit, axis=2)
        picked = jnp.sum(hit * block[None], axis=2)
        order = jnp.arange(sb, dtype=jnp.int32)
        rank = jnp.sum(valid[:, None, :] * (order[None, :] < order[:, None])[None].astype(jnp.int32), axis=2)
        chosen = valid[:, None, :] * (
            rank[:, None, :] == jnp.arange(slot_cap, dtype=jnp.int32)[None, :, None]
        ).astype(jnp.int32)
        filled = jnp.sum(chosen, axis=2)
        loc = jnp.sum(chosen * order[None, None, :], axis=2)
        tgt = jnp.sum(chosen * picked[:, None, :], axis=2)
        rows_at = jnp.where(filled > 0, chip_index * sb + loc, chips * sb)
        sums_at = jnp.where(filled > 0, tgt + tb * jnp.arange(2, dtype=jnp.int32)[:, None], 2 * tb)
        loc = jnp.where(filled > 0, loc, sb)
        return [x.reshape(-1) for x in (loc, tgt, rows_at, sums_at)]

    tiles, sums, where, masses = [], {}, [], {}

    def add(chunks):
        made = [tables_of(up, chip_at(offset)) for up, _, offset in chunks]
        joined = [jnp.concatenate([t[k] for t in made]) for k in range(4)]
        source = [x for up, low, _ in chunks for x in (up, low)]
        tile, partial = build_tiles(source, weights, joined[0], joined[1], slot_cap, sb)
        tiles.append(tile)
        where.append(joined[2:])
        for k, (_, low, offset) in enumerate(chunks):
            sums[offset % chips] = partial[k]
            masses[offset % chips] = low[sb * half :]

    up_a, up_b, down_a, down_b = upper, lower, upper, lower
    add([(upper, lower, 0)])
    far_upper = along_group(upper, 1)
    far_lower = along_group(lower, 1)
    far_at = far_upper[sb * half :, 2 * near_count].astype(jnp.int32)
    far_tiles, far_sums = build_tiles(
        (far_upper, far_lower), (own_weight,), jnp.arange(sb, dtype=jnp.int32), far_at, sb, sb
    )
    far_mass = far_lower[sb * half :]
    from_far = along_group(far_sums[0], -1)
    for step in range(1, steps + 1):
        up_a, down_b = around(up_a, 1), around(down_b, -1)
        if step < steps:
            up_b, down_a = around(up_b, 1), around(down_a, -1)
            add([(up_a, up_b, -step), (down_a, down_b, step)])
        else:
            add([(up_a, down_b, step)])
    tables = (
        jnp.concatenate([w[0] for w in where]),
        jnp.concatenate([w[1] for w in where]),
        far_at,
    )
    tiles.append(far_tiles)

    turn = jnp.asarray(spot_of, jnp.int32) - spot
    turn = jnp.where(turn < 0, turn + chips, turn)

    def by_chip(parts):
        return jnp.take(jnp.stack([parts[k] for k in range(chips)]), turn, axis=0).reshape(chips * sb, rows)

    all_mass = by_chip(masses)

    def over_chips(x):
        bit = 2
        while bit < dev_count:
            x = x + across(x, bit)
            bit *= 2
        return x

    sums[0] = sums[0] + from_far
    near_rows = by_chip(sums)
    for sweep in range(ITERS):
        if sweep > 0:
            near_rows, far_rows = row_sums(
                tables, mine, theirs, target_mass, sibling_mass, tiles, chips * sb
            )
            back = along_group(far_rows, -1)
            own = lax.dynamic_slice_in_dim(near_rows, chip * sb, sb, 0) + back
            near_rows = lax.dynamic_update_slice_in_dim(near_rows, own, chip * sb, 0)
        near_rows = over_chips(near_rows)
        own = lax.dynamic_slice_in_dim(near_rows, chip * sb, sb, 0)
        far_rows = along_group(own, 1)
        mine = column_sums(tables, near_rows, all_mass, far_rows, far_mass, tiles, 2 * tb)
        theirs = across(mine, 1)
    src_scale = source_mass / (dustbin + own)
    tgt_scale = target_mass / (dustbin + mine[:tb] + theirs[tb:])
    return (src_scale, tgt_scale)


def solution(mesh):
    placed = (
        P(("group", "dev"), None, None),
        P(("group", "dev"), None, None),
        P(("group", "dev"), None),
        P(("group", "dev"), None),
        P(("group", "dev"), None),
        P(("group", "dev"), None),
    )
    return jax.shard_map(
        local,
        mesh=mesh,
        in_specs=placed,
        out_specs=(P(("group", "dev"), None), P(("group", "dev"), None)),
        check_vma=False,
    )
```

```python
import functools

import jax
import jax.numpy as jnp
from jax import lax
from jax.experimental import pallas as pl
from jax.experimental.pallas import tpu as pltpu
from jax.sharding import PartitionSpec as P

ITERS = 2

entropic_regularizer = 0.1
dustbin = 0.5
epsilon = 1e-06

VMEM = pl.BlockSpec(memory_space=pltpu.VMEM)
SMEM = pl.BlockSpec(memory_space=pltpu.SMEM)
NT = (((1,), (1,)), ((), ()))
NN = (((1,), (0,)), ((), ()))


def split2(x):
    high = x.astype(jnp.bfloat16)
    low = (x - high.astype(jnp.float32)).astype(jnp.bfloat16)
    return high, low


def unit(x):
    return x * lax.rsqrt(jnp.mean(x * x, axis=-1, keepdims=True) + epsilon)


def stacked_parts(row):
    x = jnp.broadcast_to(row, (8, row.shape[1]))
    high = x.astype(jnp.bfloat16).astype(jnp.float32)
    rest = x - high
    low = rest.astype(jnp.bfloat16).astype(jnp.float32)
    place = lax.broadcasted_iota(jnp.int32, x.shape, 0)
    parts = jnp.where(place == 0, high, jnp.where(place == 1, low, jnp.where(place == 2, rest - low, 0.0)))
    return parts.astype(jnp.bfloat16)


def column_product(parts, tile):
    both = lax.dot_general(parts, tile, NN, preferred_element_type=jnp.float32)
    width = tile.shape[1] // 2
    return both[:, :width] + both[:, width:]


def row_product(parts, tile):
    return lax.dot_general(
        jnp.concatenate([parts, parts], axis=1), tile, NT, preferred_element_type=jnp.float32
    )


def target_kernel(emb_ref, out_ref):
    def one(block, carry):
        high, low = split2(unit(emb_ref[block]).T)
        out_ref[block] = jnp.concatenate([high, low], axis=1)
        return carry

    lax.fori_loop(0, emb_ref.shape[0], one, 0, unroll=2)


def target_operand(emb):
    blocks, rows, width = emb.shape
    return pl.pallas_call(
        target_kernel,
        out_shape=jax.ShapeDtypeStruct((blocks, width, 2 * rows), jnp.bfloat16),
        in_specs=[VMEM],
        out_specs=VMEM,
        cost_estimate=pl.CostEstimate(flops=0, bytes_accessed=3 * emb.size * 4, transcendentals=0),
        compiler_params=pltpu.CompilerParams(vmem_limit_bytes=16 << 20),
        name="target_operand",
    )(emb)


def pack_kernel(emb, mass, cand_device, cand_block, upper, lower):
    sb, rows, _ = emb.shape
    half, near = rows // 2, cand_device.shape[1]
    for block in range(sb):
        upper[block * half : (block + 1) * half] = emb[block, 0:half]
        lower[block * half : (block + 1) * half] = emb[block, half:rows]
    upper[sb * half :] = jnp.zeros((sb, emb.shape[2]), jnp.float32)
    upper[sb * half :, 0:near] = cand_device[...].astype(jnp.float32)
    upper[sb * half :, near : near + cand_block.shape[1]] = cand_block[...].astype(jnp.float32)
    lower[sb * half :] = mass[...]


def pack(emb, mass, cand_device, cand_block):
    sb, rows, width = emb.shape
    shape = jax.ShapeDtypeStruct((sb * (rows // 2 + 1), width), jnp.float32)
    return pl.pallas_call(
        pack_kernel,
        out_shape=(shape, shape),
        in_specs=[VMEM] * 4,
        out_specs=(VMEM, VMEM),
        compiler_params=pltpu.CompilerParams(vmem_limit_bytes=16 << 20),
        name="pack",
    )(emb, mass, cand_device, cand_block)


def chip_at(chips, chip, offset):
    odd = lax.rem(chip, 2)
    spot = jnp.where(odd == 1, chips - 1 - chip // 2, chip // 2) + offset
    spot = jnp.where(spot < 0, spot + chips, jnp.where(spot >= chips, spot - chips, spot))
    return jnp.where(spot < chips // 2, 2 * spot, 2 * chips - 1 - 2 * spot)


def tile_kernel(plan, *refs):
    chunks, slots, sb, half, tb, near, offsets, far, chained, closing = plan
    sides = 1 if far else 2
    refs = list(refs)
    device = refs.pop(0)
    source = [refs.pop(0) for _ in range(2 * chunks)]
    weight = [refs.pop(0) for _ in range(sides)]
    rows_in, mass_in = (refs.pop(0), refs.pop(0)) if chained else (None, None)
    back = refs.pop(0) if closing else None
    tiles, table, rows_out, mass_out, partial, staged, named, listed, arrived = refs
    count = chunks * sides * slots
    width = source[0].shape[1]
    scale = 1.0 / (width * entropic_regularizer)
    me = device[0]
    chips = rows_out.shape[0] // sb

    for chunk in range(chunks):
        staged[chunk * sb : (chunk + 1) * sb] = source[2 * chunk][sb * half :].astype(jnp.int32)
    copy = pltpu.make_async_copy(staged, named, arrived)
    copy.start()
    if chained:
        rows_out[...] = rows_in[...]
        mass_out[...] = mass_in[...]
    partial[...] = jnp.zeros_like(partial)
    place = lax.broadcasted_iota(jnp.int32, (8, 2 * width), 0)
    ones = jnp.where(place == 0, 1.0, 0.0).astype(jnp.bfloat16)
    copy.wait()

    chip_of = []
    for chunk in range(chunks):
        at_chip = jnp.int32(0) if far else chip_at(chips, me // 2, offsets[chunk])
        chip_of.append(at_chip)
        for side in range(sides):
            base = (chunk * sides + side) * slots
            if far:
                for j in range(sb):
                    listed[base + j] = j
                    table[j] = named[j, 2 * near]
                continue
            wanted = me if side == 0 else me + 1 - 2 * lax.rem(me, 2)
            filled = jnp.int32(0)
            for block in range(sb):
                found, which = jnp.int32(0), jnp.int32(0)
                for k in range(near):
                    hit = named[chunk * sb + block, k] == wanted
                    found = jnp.where(hit, 1, found)
                    which = jnp.where(hit, named[chunk * sb + block, near + k], which)
                listed[base + filled] = block
                table[count + base + filled] = which
                filled = filled + found
            for j in range(slots):
                valid = j < filled
                block = jnp.where(valid, listed[base + j], sb)
                which = jnp.where(valid, table[count + base + j], 2 * tb)
                listed[base + j] = block
                table[base + j] = jnp.where(valid, at_chip * sb + block, chips * sb)
                table[count + base + j] = jnp.where(valid, which + side * tb, 2 * tb)

    for chunk in range(chunks):
        upper, lower = source[2 * chunk], source[2 * chunk + 1]
        for side in range(sides):
            for j in range(slots):
                at = (chunk * sides + side) * slots + j
                block = listed[at]
                start = pl.multiple_of(lax.rem(block, sb) * half, half)
                left = jnp.concatenate([upper[pl.ds(start, half)], lower[pl.ds(start, half)]], axis=0)
                high, low = split2(unit(left))
                right = weight[side][table[at] if far else lax.rem(table[count + at], tb)]
                both = lax.dot_general(
                    jnp.concatenate([high, low], axis=1),
                    jnp.concatenate([right, right], axis=0),
                    NN,
                    preferred_element_type=jnp.float32,
                )
                nodes = both.shape[1] // 2
                affinity = both[:, :nodes] + both[:, nodes:]
                tile = jnp.exp(affinity * scale) * (1.0 / (8.0 * nodes))
                tile = jnp.concatenate(split2(tile), axis=1)
                tiles[at] = tile
                spot = chunk * (sb + 1) + block
                partial[spot] += lax.dot_general(ones, tile, NT, preferred_element_type=jnp.float32)
        start = pl.multiple_of(chip_of[chunk] * sb, sb)
        for block in range(sb):
            rows_out[pl.ds(start + block, 1)] = partial[chunk * (sb + 1) + block][0:1]
        mass_out[pl.ds(start, sb)] = lower[sb * half :]
    if closing:
        start = pl.multiple_of(me // 2 * sb, sb)
        rows_out[pl.ds(start, sb)] += back[...]


def build_tiles(device, source, weight, slots, sb, near, chips, offsets=(), chain=(), back=None):
    chunks, sides, far = len(source) // 2, len(weight), not offsets
    half, width = source[0].shape[0] // sb - 1, source[0].shape[1]
    tb, nodes = weight[0].shape[0], weight[0].shape[2] // 2
    count = chunks * sides * slots
    plan = (chunks, slots, sb, half, tb, near, offsets, far, bool(chain), back is not None)
    operands = [device, *source, *weight, *chain] + ([] if back is None else [back])
    rows = jax.ShapeDtypeStruct(((1 if far else chips) * sb, 2 * half), jnp.float32)
    return pl.pallas_call(
        functools.partial(tile_kernel, plan),
        out_shape=(
            jax.ShapeDtypeStruct((count, 2 * half, 2 * nodes), jnp.bfloat16),
            jax.ShapeDtypeStruct((count if far else 2 * count + 1,), jnp.int32),
            rows,
            rows,
        ),
        in_specs=[SMEM] + [VMEM] * (len(operands) - 1),
        out_specs=(VMEM, SMEM, VMEM, VMEM),
        scratch_shapes=[
            pltpu.VMEM((chunks * (sb + 1), 8, 2 * half), jnp.float32),
            pltpu.VMEM((chunks * sb, width), jnp.int32),
            pltpu.SMEM((chunks * sb, width), jnp.int32),
            pltpu.SMEM((count + 1,), jnp.int32),
            pltpu.SemaphoreType.DMA,
        ],
        cost_estimate=pl.CostEstimate(
            flops=count * 2 * half * nodes * width * 8,
            bytes_accessed=count * 2 * half * nodes * 4 + sides * weight[0].size * 2,
            transcendentals=count * 2 * half * nodes,
        ),
        compiler_params=pltpu.CompilerParams(vmem_limit_bytes=16 << 20),
        name="build_tiles",
    )(*operands)


def column_kernel(near, far, *refs):
    refs = list(refs)
    device = refs.pop(0)
    tables = [refs.pop(0) for _ in near]
    far_at, rows, mass, far_rows, far_mass = [refs.pop(0) for _ in range(5)]
    tiles = [refs.pop(0) for _ in range(len(near) + 1)]
    out, src_out, scale, total = refs
    count, sb = rows.shape[0], src_out.shape[0]
    scale[...] = jnp.zeros_like(scale)
    scale[0:count] = mass[...] / (dustbin + rows[...])
    scale[count + 8 : count + 8 + far] = far_mass[...] / (dustbin + far_rows[...])
    total[...] = jnp.zeros_like(total)
    for part, slots in enumerate(near):
        for slot in range(slots):
            parts = stacked_parts(scale[pl.ds(tables[part][slot], 1), :])
            total[tables[part][slots + slot]] += column_product(parts, tiles[part][slot])
    for slot in range(far):
        parts = stacked_parts(scale[count + 8 + slot : count + 9 + slot, :])
        total[far_at[slot]] += column_product(parts, tiles[len(near)][slot])
    for block in range(out.shape[0]):
        out[block : block + 1] = jnp.sum(total[block], axis=0, keepdims=True)
    src_out[...] = scale[pl.ds(pl.multiple_of(device[0] // 2 * sb, sb), sb)]


def column_sums(device, tables, far_at, rows, mass, far_rows, far_mass, tiles, targets):
    near = tuple(t.shape[0] for t in tiles[:-1])
    far, nodes = tiles[-1].shape[0], tiles[-1].shape[2] // 2
    width = rows.shape[1]
    return pl.pallas_call(
        functools.partial(column_kernel, near, far),
        out_shape=(
            jax.ShapeDtypeStruct((targets, nodes), jnp.float32),
            jax.ShapeDtypeStruct(far_rows.shape, jnp.float32),
        ),
        in_specs=[SMEM] * (2 + len(tables)) + [VMEM] * (4 + len(tiles)),
        out_specs=(VMEM, VMEM),
        scratch_shapes=[
            pltpu.VMEM((rows.shape[0] + 8 + (far + 7) // 8 * 8, width), jnp.float32),
            pltpu.VMEM((targets + 1, 8, nodes), jnp.float32),
        ],
        cost_estimate=pl.CostEstimate(
            flops=sum(t.size for t in tiles) * 16, bytes_accessed=sum(t.size for t in tiles) * 2, transcendentals=0
        ),
        compiler_params=pltpu.CompilerParams(vmem_limit_bytes=16 << 20),
        name="column_sums",
    )(device, *tables, far_at, rows, mass, far_rows, far_mass, *tiles)


def row_kernel(near, far, *refs):
    refs = list(refs)
    tables = [refs.pop(0) for _ in near]
    far_at, mine, theirs, mass, other_mass = [refs.pop(0) for _ in range(5)]
    tiles = [refs.pop(0) for _ in range(len(near) + 1)]
    out, far_out, scale, total = refs
    blocks = mass.shape[0]
    scale[2 * blocks :] = jnp.zeros((8, scale.shape[1]), jnp.float32)
    scale[0:blocks] = mass[...] / (dustbin + mine[0:blocks] + theirs[blocks : 2 * blocks])
    scale[blocks : 2 * blocks] = other_mass[...] / (dustbin + mine[blocks : 2 * blocks] + theirs[0:blocks])
    total[...] = jnp.zeros_like(total)
    for part, slots in enumerate(near):
        for slot in range(slots):
            parts = stacked_parts(scale[pl.ds(tables[part][slots + slot], 1), :])
            total[tables[part][slot]] += row_product(parts, tiles[part][slot])
    for slot in range(far):
        parts = stacked_parts(scale[pl.ds(far_at[slot], 1), :])
        far_out[slot : slot + 1] = jnp.sum(row_product(parts, tiles[len(near)][slot]), axis=0, keepdims=True)
    for block in range(out.shape[0]):
        out[block : block + 1] = jnp.sum(total[block], axis=0, keepdims=True)


def row_sums(tables, far_at, mine, theirs, mass, other_mass, tiles, sources):
    near = tuple(t.shape[0] for t in tiles[:-1])
    far, nodes = tiles[-1].shape[0], tiles[-1].shape[2] // 2
    width = tiles[-1].shape[1]
    return pl.pallas_call(
        functools.partial(row_kernel, near, far),
        out_shape=(
            jax.ShapeDtypeStruct((sources, width), jnp.float32),
            jax.ShapeDtypeStruct((far, width), jnp.float32),
        ),
        in_specs=[SMEM] * (1 + len(tables)) + [VMEM] * (4 + len(tiles)),
        out_specs=(VMEM, VMEM),
        scratch_shapes=[
            pltpu.VMEM((mine.shape[0] + 8, nodes), jnp.float32),
            pltpu.VMEM((sources + 1, 8, width), jnp.float32),
        ],
        cost_estimate=pl.CostEstimate(
            flops=sum(t.size for t in tiles) * 16, bytes_accessed=sum(t.size for t in tiles) * 2, transcendentals=0
        ),
        compiler_params=pltpu.CompilerParams(vmem_limit_bytes=16 << 20),
        name="row_sums",
    )(*tables, far_at, mine, theirs, mass, other_mass, *tiles)


def after(x, *others):
    return lax.optimization_barrier((x, *others))[0]


def local(source_emb, target_emb, source_mass, target_mass, cand_device, cand_block):
    dev_count = lax.axis_size("dev")
    group_count = lax.axis_size("group")
    chips = dev_count // 2
    sb, tb = source_emb.shape[0], target_emb.shape[0]
    near = cand_device.shape[1]
    slot_cap = (near * sb + dev_count - 1) // dev_count + 1
    steps = chips // 2
    ring = list(range(0, chips, 2)) + list(range(chips - 1, 0, -2))

    def around(x, by):
        pairs = [
            (2 * ring[i] + core, 2 * ring[(i + by) % chips] + core) for i in range(chips) for core in range(2)
        ]
        return lax.ppermute(x, "dev", pairs)

    def across(x, bit):
        return lax.ppermute(x, "dev", [(i, i ^ bit) for i in range(dev_count)])

    def to_group(x, by, bit=0):
        pairs = [
            (g * dev_count + i, (g + by) % group_count * dev_count + (i ^ bit))
            for g in range(group_count)
            for i in range(dev_count)
        ]
        return lax.ppermute(x, ("group", "dev"), pairs)

    device = lax.axis_index("dev").astype(jnp.int32)
    me = device.reshape(1)
    chip = device // 2

    def own_rows(x, bit=0):
        return lax.dynamic_slice_in_dim(x, ((device ^ bit) // 2) * sb, sb, 0)

    def add_rows(x, part, bit=0):
        return lax.dynamic_update_slice_in_dim(x, own_rows(x, bit) + part, ((device ^ bit) // 2) * sb, 0)

    upper, lower = pack(source_emb, source_mass, cand_device, cand_block)
    up_a, up_b, down_a, down_b = upper, lower, upper, lower
    tiles, tables, chain = [], [], ()
    build = functools.partial(build_tiles, me, sb=sb, near=near, chips=chips)

    def add(chunks, chain, back=None):
        tile, table, *chain = build(
            [x for up, low, _ in chunks for x in (up, low)],
            weights,
            slots=slot_cap,
            offsets=tuple(offset for _, _, offset in chunks),
            chain=chain,
            back=back,
        )
        tiles.append(tile)
        tables.append(table)
        return chain

    waiting = []
    for step in range(1, steps + 1):
        if step == 2:
            own_weight = target_operand(target_emb)
            up_a, down_b, own_weight = lax.optimization_barrier((up_a, down_b, own_weight))
        if step == 3:
            sibling_weight = target_operand(sibling_emb)
            up_a, down_b, sibling_weight = lax.optimization_barrier((up_a, down_b, sibling_weight))
            weights = (own_weight, sibling_weight)
        if step > 3:
            chain = add(waiting.pop(0), chain)
            up_a, down_b, *chain = lax.optimization_barrier((up_a, down_b, *chain))
        up_a, down_b = around(up_a, 1), around(down_b, -1)
        if step == 1:
            sibling_emb = across(target_emb, 1)
            sibling_mass = across(target_mass, 1)
            far_upper = to_group(upper, 1)
            far_lower = to_group(lower, 1)
        if step == 3:
            chain = add([(upper, lower, 0)], chain)
            far_tiles, far_at, far_sums, far_mass = build((far_upper, far_lower), (own_weight,), slots=sb)
            up_b, down_a, *chain = lax.optimization_barrier((up_b, down_a, *chain, far_sums))
            far_sums = chain.pop()
            from_far = to_group(far_sums, -1)
        if step < steps:
            up_b, down_a = around(up_b, 1), around(down_a, -1)
            waiting.append([(up_a, up_b, -step), (down_a, down_b, step)])
    for chunks in waiting:
        chain = add(chunks, chain)
    near_rows, all_mass = add([(up_a, down_b, steps)], chain, from_far)
    tiles.append(far_tiles)

    last = dev_count // 2
    for sweep in range(ITERS):
        if sweep > 0:
            near_rows, far_rows = row_sums(
                tables, far_at, mine, theirs, target_mass, sibling_mass, tiles, chips * sb
            )
            to_own, to_next = to_group(far_rows, -1), to_group(far_rows, -1, 2)
        bit = 2
        while bit < dev_count:
            if bit == last:
                far_rows = to_group(own_rows(near_rows), 1)
                far_rows = far_rows + to_group(own_rows(near_rows, last), 1, last)
            near_rows = near_rows + across(near_rows, bit)
            if sweep > 0 and bit == 2:
                near_rows = add_rows(add_rows(near_rows, to_own), to_next, 2)
            bit *= 2
        mine, src_scale = column_sums(
            me, tables, far_at, near_rows, all_mass, far_rows, far_mass, tiles, 2 * tb
        )
        theirs = across(mine, 1)
    tgt_scale = target_mass / (dustbin + mine[:tb] + theirs[tb:])
    return (src_scale, tgt_scale)


def solution(mesh):
    placed = (
        P(("group", "dev"), None, None),
        P(("group", "dev"), None, None),
        P(("group", "dev"), None),
        P(("group", "dev"), None),
        P(("group", "dev"), None),
        P(("group", "dev"), None),
    )
    return jax.shard_map(
        local,
        mesh=mesh,
        in_specs=placed,
        out_specs=(P(("group", "dev"), None), P(("group", "dev"), None)),
        check_vma=False,
    )
```

```python
import functools
import math

import jax
import jax.numpy as jnp
from jax import lax
from jax.experimental import pallas as pl
from jax.experimental.pallas import tpu as pltpu
from jax.sharding import PartitionSpec as P

ITERS = 2

entropic_regularizer = 0.1
dustbin = 0.5
epsilon = 1e-06

VMEM = pl.BlockSpec(memory_space=pltpu.VMEM)
SMEM = pl.BlockSpec(memory_space=pltpu.SMEM)
HBM = pl.BlockSpec(memory_space=pltpu.HBM)
LIGHT = pl.CostEstimate(flops=1, bytes_accessed=1, transcendentals=0)
NT = (((1,), (1,)), ((), ()))
NN = (((1,), (0,)), ((), ()))


def in_vmem(*arrays):
    return [pltpu.with_memory_space_constraint(x, pltpu.VMEM) for x in arrays]


def in_hbm(*arrays):
    return [pltpu.with_memory_space_constraint(x, pltpu.HBM) for x in arrays]


def split2(x):
    high = x.astype(jnp.bfloat16)
    low = (x - high.astype(jnp.float32)).astype(jnp.bfloat16)
    return high, low


def unit(x):
    return x * lax.rsqrt(jnp.mean(x * x, axis=-1, keepdims=True) + epsilon)


def stacked_parts(row):
    x = jnp.broadcast_to(row, (8, row.shape[1]))
    high = x.astype(jnp.bfloat16).astype(jnp.float32)
    rest = x - high
    low = rest.astype(jnp.bfloat16).astype(jnp.float32)
    place = lax.broadcasted_iota(jnp.int32, x.shape, 0)
    parts = jnp.where(place == 0, high, jnp.where(place == 1, low, jnp.where(place == 2, rest - low, 0.0)))
    return parts.astype(jnp.bfloat16)


def column_product(parts, tile):
    both = lax.dot_general(parts, tile, NN, preferred_element_type=jnp.float32)
    width = tile.shape[1] // 2
    return both[:, :width] + both[:, width:]


def row_product(parts, tile):
    return lax.dot_general(
        jnp.concatenate([parts, parts], axis=1), tile, NT, preferred_element_type=jnp.float32
    )


def target_kernel(emb_ref, out_ref, staged, arrived):
    parts = arrived.shape[0]
    share = emb_ref.shape[0] // parts
    copies = []
    for part in range(parts):
        spots = pl.ds(part * share, share)
        copies.append(pltpu.make_async_copy(emb_ref.at[spots], staged.at[spots], arrived.at[part]))
        copies[-1].start()

    def one(block, carry):
        high, low = split2(unit(staged[block]).T)
        out_ref[block] = jnp.concatenate([high, low], axis=1)
        return carry

    for part in range(parts):
        copies[part].wait()
        lax.fori_loop(part * share, (part + 1) * share, one, 0, unroll=4)


def target_operand(emb):
    blocks, rows, width = emb.shape
    parts = math.gcd(blocks, 8)
    return pl.pallas_call(
        target_kernel,
        out_shape=pltpu.VMEM((blocks, width, 2 * rows), jnp.bfloat16),
        in_specs=[pl.BlockSpec(memory_space=pl.ANY)],
        out_specs=VMEM,
        scratch_shapes=[pltpu.VMEM(emb.shape, jnp.float32), pltpu.SemaphoreType.DMA((parts,))],
        cost_estimate=LIGHT,
        compiler_params=pltpu.CompilerParams(vmem_limit_bytes=16 << 20),
        name="target_operand",
    )(emb)


def pack_kernel(device, emb, mass, cand_device, cand_block, upper, lower, both, named, blocks, arrived):
    sb, rows, width = emb.shape
    half, near = rows // 2, cand_device.shape[1]
    copies = [
        pltpu.make_async_copy(cand_device, named, arrived.at[0]),
        pltpu.make_async_copy(cand_block, blocks, arrived.at[1]),
        pltpu.make_async_copy(mass, lower.at[pl.ds(sb * half, sb)], arrived.at[2]),
    ]
    for block in range(sb):
        into = pl.ds(block * half, half)
        copies.append(pltpu.make_async_copy(emb.at[block, pl.ds(0, half)], upper.at[into], arrived.at[3 + 2 * block]))
        copies.append(
            pltpu.make_async_copy(emb.at[block, pl.ds(half, half)], lower.at[into], arrived.at[4 + 2 * block])
        )
    for copy in copies:
        copy.start()
    for copy in copies[:2]:
        copy.wait()
    upper[sb * half :] = jnp.zeros((sb, width), jnp.float32)
    upper[sb * half :, 0:near] = named[...].astype(jnp.float32)
    upper[sb * half :, near : near + blocks.shape[1]] = blocks[...].astype(jnp.float32)
    for copy in copies[2:]:
        copy.wait()
    count = upper.shape[0]
    both[0:count] = upper[...]
    both[count:] = lower[...]


def pack(device, emb, mass, cand_device, cand_block):
    sb, rows, width = emb.shape
    count = sb * (rows // 2 + 1)
    shape = pltpu.VMEM((count, width), jnp.float32)
    return pl.pallas_call(
        pack_kernel,
        out_shape=(shape, shape, pltpu.VMEM((2 * count, width), jnp.float32)),
        in_specs=[SMEM] + [HBM] * 4,
        out_specs=(VMEM, VMEM, VMEM),
        scratch_shapes=[
            pltpu.VMEM(cand_device.shape, jnp.int32),
            pltpu.VMEM(cand_block.shape, jnp.int32),
            pltpu.SemaphoreType.DMA((3 + 2 * sb,)),
        ],
        compiler_params=pltpu.CompilerParams(vmem_limit_bytes=16 << 20),
        name="pack",
    )(device, *in_hbm(emb, mass, cand_device, cand_block))


def chip_at(chips, chip, offset):
    odd = lax.rem(chip, 2)
    spot = jnp.where(odd == 1, chips - 1 - chip // 2, chip // 2) + offset
    spot = jnp.where(spot < 0, spot + chips, jnp.where(spot >= chips, spot - chips, spot))
    return jnp.where(spot < chips // 2, 2 * spot, 2 * chips - 1 - 2 * spot)


def tile_kernel(plan, *refs):
    chunks, slots, sb, half, tb, near, offsets, far, chained, closing = plan
    sides = 1 if far else 2
    refs = list(refs)
    device = refs.pop(0)
    if far:
        both = refs.pop(0)
        source = [both.at[pl.ds(start, sb * (half + 1))] for start in (0, sb * (half + 1))]
    else:
        source = [refs.pop(0) for _ in range(2 * chunks)]
    weight = [refs.pop(0) for _ in range(sides)]
    rows_in, mass_in = (refs.pop(0), refs.pop(0)) if chained else (None, None)
    back = refs.pop(0) if closing else None
    tiles, table, rows_out, mass_out, partial, staged, named, listed, arrived = refs
    count = chunks * sides * slots
    width = source[0].shape[1]
    scale = 1.0 / (width * entropic_regularizer)
    me = device[0]
    chips = rows_out.shape[0] // sb

    for chunk in range(chunks):
        staged[chunk * sb : (chunk + 1) * sb] = source[2 * chunk][sb * half :].astype(jnp.int32)
    copy = pltpu.make_async_copy(staged, named, arrived)
    copy.start()
    if chained:
        rows_out[...] = rows_in[...]
        mass_out[...] = mass_in[...]
    partial[...] = jnp.zeros_like(partial)
    place = lax.broadcasted_iota(jnp.int32, (8, 2 * width), 0)
    ones = jnp.where(place == 0, 1.0, 0.0).astype(jnp.bfloat16)
    copy.wait()

    chip_of = []
    for chunk in range(chunks):
        at_chip = jnp.int32(0) if far else chip_at(chips, me // 2, offsets[chunk])
        chip_of.append(at_chip)
        for side in range(sides):
            base = (chunk * sides + side) * slots
            if far:
                for j in range(sb):
                    listed[base + j] = j
                    table[j] = named[j, 2 * near]
                continue
            wanted = me if side == 0 else me + 1 - 2 * lax.rem(me, 2)
            filled = jnp.int32(0)
            for block in range(sb):
                found, which = jnp.int32(0), jnp.int32(0)
                for k in range(near):
                    hit = named[chunk * sb + block, k] == wanted
                    found = jnp.where(hit, 1, found)
                    which = jnp.where(hit, named[chunk * sb + block, near + k], which)
                listed[base + filled] = block
                table[count + base + filled] = which
                filled = filled + found
            for j in range(slots):
                valid = j < filled
                block = jnp.where(valid, listed[base + j], sb)
                which = jnp.where(valid, table[count + base + j], 2 * tb)
                listed[base + j] = block
                table[base + j] = jnp.where(valid, at_chip * sb + block, chips * sb)
                table[count + base + j] = jnp.where(valid, which + side * tb, 2 * tb)

    for chunk in range(chunks):
        upper, lower = source[2 * chunk], source[2 * chunk + 1]
        for side in range(sides):
            for j in range(slots):
                at = (chunk * sides + side) * slots + j
                block = listed[at]
                start = pl.multiple_of(lax.rem(block, sb) * half, half)
                left = jnp.concatenate([upper[pl.ds(start, half)], lower[pl.ds(start, half)]], axis=0)
                high, low = split2(unit(left))
                right = weight[side][table[at] if far else lax.rem(table[count + at], tb)]
                both = lax.dot_general(
                    jnp.concatenate([high, low], axis=1),
                    jnp.concatenate([right, right], axis=0),
                    NN,
                    preferred_element_type=jnp.float32,
                )
                nodes = both.shape[1] // 2
                affinity = both[:, :nodes] + both[:, nodes:]
                tile = jnp.exp(affinity * scale) * (1.0 / (8.0 * nodes))
                tile = jnp.concatenate(split2(tile), axis=1)
                tiles[at] = tile
                spot = chunk * (sb + 1) + block
                partial[spot] += lax.dot_general(ones, tile, NT, preferred_element_type=jnp.float32)
        start = pl.multiple_of(chip_of[chunk] * sb, sb)
        for block in range(sb):
            rows_out[pl.ds(start + block, 1)] = partial[chunk * (sb + 1) + block][0:1]
        mass_out[pl.ds(start, sb)] = lower[sb * half :]
    if closing:
        start = pl.multiple_of(me // 2 * sb, sb)
        rows_out[pl.ds(start, sb)] += back[...]


def build_tiles(device, source, weight, slots, sb, near, chips, offsets=(), chain=(), back=None):
    chunks, sides, far = max(1, len(source) // 2), len(weight), not offsets
    half, width = source[0].shape[0] // (sb * (1 + far)) - 1, source[0].shape[1]
    tb, nodes = weight[0].shape[0], weight[0].shape[2] // 2
    count = chunks * sides * slots
    plan = (chunks, slots, sb, half, tb, near, offsets, far, bool(chain), back is not None)
    operands = [device, *source, *in_vmem(*weight), *chain] + ([] if back is None else [back])
    rows = jax.ShapeDtypeStruct(((1 if far else chips) * sb, 2 * half), jnp.float32)
    return pl.pallas_call(
        functools.partial(tile_kernel, plan),
        out_shape=(
            pltpu.VMEM((count, 2 * half, 2 * nodes), jnp.bfloat16),
            jax.ShapeDtypeStruct((count if far else 2 * count + 1,), jnp.int32),
            rows,
            rows,
        ),
        in_specs=[SMEM] + [VMEM] * (len(operands) - 1),
        out_specs=(VMEM, SMEM, VMEM, VMEM),
        scratch_shapes=[
            pltpu.VMEM((chunks * (sb + 1), 8, 2 * half), jnp.float32),
            pltpu.VMEM((chunks * sb, width), jnp.int32),
            pltpu.SMEM((chunks * sb, width), jnp.int32),
            pltpu.SMEM((count + 1,), jnp.int32),
            pltpu.SemaphoreType.DMA,
        ],
        cost_estimate=LIGHT,
        compiler_params=pltpu.CompilerParams(vmem_limit_bytes=16 << 20),
        name="build_tiles",
    )(*operands)


SMALL = pltpu.CompilerParams(vmem_limit_bytes=16 << 20)


def add_kernel(device, mine, theirs, total, own):
    sb = own.shape[0]
    total[...] = mine[...] + theirs[...]
    own[...] = total[pl.ds(pl.multiple_of(device[0] // 2 * sb, sb), sb)]


def add_last(device, mine, theirs, sb):
    return pl.pallas_call(
        add_kernel,
        out_shape=(
            jax.ShapeDtypeStruct(mine.shape, jnp.float32),
            jax.ShapeDtypeStruct((sb, mine.shape[1]), jnp.float32),
        ),
        in_specs=[SMEM, VMEM, VMEM],
        out_specs=(VMEM, VMEM),
        compiler_params=SMALL,
        name="add_last",
    )(device, mine, theirs)


def insert_kernel(device, rows, part, out):
    out[...] = rows[...]
    out[pl.ds(pl.multiple_of(device[0] // 2 * part.shape[0], part.shape[0]), part.shape[0])] += part[...]


def add_own(device, rows, part):
    return pl.pallas_call(
        insert_kernel,
        out_shape=jax.ShapeDtypeStruct(rows.shape, jnp.float32),
        in_specs=[SMEM, VMEM, VMEM],
        out_specs=VMEM,
        compiler_params=SMALL,
        name="add_own",
    )(device, rows, part)


def column_kernel(counts, *refs):
    refs = list(refs)
    tables = [refs.pop(0) for _ in counts]
    rows, mass = refs.pop(0), refs.pop(0)
    tiles = [refs.pop(0) for _ in counts]
    out, scale, total = refs
    count = rows.shape[0]
    scale[0:count] = mass[...] / (dustbin + rows[...])
    scale[count:] = jnp.zeros((8, scale.shape[1]), jnp.float32)
    total[...] = jnp.zeros_like(total)
    for part, slots in enumerate(counts):
        for slot in range(slots):
            parts = stacked_parts(scale[pl.ds(tables[part][slot], 1), :])
            total[tables[part][slots + slot]] += column_product(parts, tiles[part][slot])
    for block in range(out.shape[0]):
        out[block : block + 1] = jnp.sum(total[block], axis=0, keepdims=True)


def column_sums(tables, rows, mass, tiles, targets):
    counts = tuple(t.shape[0] for t in tiles)
    width, nodes = rows.shape[1], tiles[0].shape[2] // 2
    return pl.pallas_call(
        functools.partial(column_kernel, counts),
        out_shape=jax.ShapeDtypeStruct((targets, nodes), jnp.float32),
        in_specs=[SMEM] * len(tables) + [VMEM] * (2 + len(tiles)),
        out_specs=VMEM,
        scratch_shapes=[
            pltpu.VMEM((rows.shape[0] + 8, width), jnp.float32),
            pltpu.VMEM((targets + 1, 8, nodes), jnp.float32),
        ],
        cost_estimate=LIGHT,
        compiler_params=SMALL,
        name="column_sums",
    )(*tables, rows, mass, *in_vmem(*tiles))


def far_column_kernel(far_at, sums, far_rows, far_mass, tiles, out, scale):
    far = tiles.shape[0]
    out[...] = sums[...]
    scale[...] = far_mass[...] / (dustbin + far_rows[...])
    for slot in range(far):
        product = column_product(stacked_parts(scale[slot : slot + 1, :]), tiles[slot])
        out[pl.ds(far_at[slot], 1)] += jnp.sum(product, axis=0, keepdims=True)


def far_column_sums(far_at, sums, far_rows, far_mass, tiles):
    return pl.pallas_call(
        far_column_kernel,
        out_shape=jax.ShapeDtypeStruct(sums.shape, jnp.float32),
        in_specs=[SMEM] + [VMEM] * 4,
        out_specs=VMEM,
        scratch_shapes=[pltpu.VMEM(far_mass.shape, jnp.float32)],
        cost_estimate=LIGHT,
        compiler_params=SMALL,
        name="far_column_sums",
    )(far_at, sums, far_rows, far_mass, *in_vmem(tiles))


def scale_kernel(rows, mass, mine, theirs, target_mass, src, tgt):
    blocks = tgt.shape[0]
    src[...] = mass[...] / (dustbin + rows[...])
    tgt[...] = target_mass[...] / (dustbin + mine[0:blocks] + theirs[blocks : 2 * blocks])


def scales(rows, mass, mine, theirs, target_mass):
    return pl.pallas_call(
        scale_kernel,
        out_shape=(
            jax.ShapeDtypeStruct(mass.shape, jnp.float32),
            jax.ShapeDtypeStruct(target_mass.shape, jnp.float32),
        ),
        in_specs=[VMEM] * 5,
        out_specs=(VMEM, VMEM),
        compiler_params=SMALL,
        name="scales",
    )(rows, mass, mine, theirs, target_mass)


def far_row_kernel(far_at, mine, theirs, mass, tiles, out, scale):
    blocks = mass.shape[0]
    scale[...] = mass[...] / (dustbin + mine[0:blocks] + theirs[blocks : 2 * blocks])
    for slot in range(tiles.shape[0]):
        product = row_product(stacked_parts(scale[pl.ds(far_at[slot], 1), :]), tiles[slot])
        out[slot : slot + 1] = jnp.sum(product, axis=0, keepdims=True)


def far_row_sums(far_at, mine, theirs, mass, tiles):
    return pl.pallas_call(
        far_row_kernel,
        out_shape=jax.ShapeDtypeStruct(tiles.shape[:2], jnp.float32),
        in_specs=[SMEM] + [VMEM] * 4,
        out_specs=VMEM,
        scratch_shapes=[pltpu.VMEM(mass.shape, jnp.float32)],
        cost_estimate=LIGHT,
        compiler_params=SMALL,
        name="far_row_sums",
    )(far_at, mine, theirs, mass, *in_vmem(tiles))


def row_kernel(counts, *refs):
    refs = list(refs)
    tables = [refs.pop(0) for _ in counts]
    mine, theirs, mass, other_mass = [refs.pop(0) for _ in range(4)]
    tiles = [refs.pop(0) for _ in counts]
    out, scale, total = refs
    blocks = mass.shape[0]
    scale[0:blocks] = mass[...] / (dustbin + mine[0:blocks] + theirs[blocks : 2 * blocks])
    scale[blocks : 2 * blocks] = other_mass[...] / (dustbin + mine[blocks : 2 * blocks] + theirs[0:blocks])
    scale[2 * blocks :] = jnp.zeros((8, scale.shape[1]), jnp.float32)
    total[...] = jnp.zeros_like(total)
    for part, slots in enumerate(counts):
        for slot in range(slots):
            parts = stacked_parts(scale[pl.ds(tables[part][slots + slot], 1), :])
            total[tables[part][slot]] += row_product(parts, tiles[part][slot])
    for block in range(out.shape[0]):
        out[block : block + 1] = jnp.sum(total[block], axis=0, keepdims=True)


def row_sums(tables, mine, theirs, mass, other_mass, tiles, sources):
    counts = tuple(t.shape[0] for t in tiles)
    width, nodes = tiles[0].shape[1], tiles[0].shape[2] // 2
    return pl.pallas_call(
        functools.partial(row_kernel, counts),
        out_shape=jax.ShapeDtypeStruct((sources, width), jnp.float32),
        in_specs=[SMEM] * len(tables) + [VMEM] * (4 + len(tiles)),
        out_specs=VMEM,
        scratch_shapes=[
            pltpu.VMEM((mine.shape[0] + 8, nodes), jnp.float32),
            pltpu.VMEM((sources + 1, 8, width), jnp.float32),
        ],
        cost_estimate=LIGHT,
        compiler_params=SMALL,
        name="row_sums",
    )(*tables, mine, theirs, mass, other_mass, *in_vmem(*tiles))


def local(source_emb, target_emb, source_mass, target_mass, cand_device, cand_block):
    dev_count = lax.axis_size("dev")
    group_count = lax.axis_size("group")
    chips = dev_count // 2
    sb, tb = source_emb.shape[0], target_emb.shape[0]
    near = cand_device.shape[1]
    slot_cap = (near * sb + dev_count - 1) // dev_count + 1
    steps = chips // 2
    ring = list(range(0, chips, 2)) + list(range(chips - 1, 0, -2))

    def around(x, by):
        pairs = [
            (2 * ring[i] + core, 2 * ring[(i + by) % chips] + core) for i in range(chips) for core in range(2)
        ]
        return lax.ppermute(x, "dev", pairs)

    def across(x, bit):
        return lax.ppermute(x, "dev", [(i, i ^ bit) for i in range(dev_count)])

    def to_group(x, by):
        return lax.ppermute(x, "group", [(g, (g + by) % group_count) for g in range(group_count)])

    device = lax.axis_index("dev").astype(jnp.int32)
    me = device.reshape(1)

    upper, lower, both = pack(me, source_emb, source_mass, cand_device, cand_block)
    sibling_emb, sibling_mass = across(target_emb, 1), across(target_mass, 1)
    far_both = [both]

    weights, tiles, tables, chain, far_parts = [], [], [], [], []
    build = functools.partial(build_tiles, me, sb=sb, near=near, chips=chips)

    def target_job(emb):
        weights.append(target_operand(emb))
        return weights[-1]

    def near_job(chunks, back=None):
        tile, table, *passed = build(
            [x for up, low, _ in chunks for x in (up, low)],
            weights,
            slots=slot_cap,
            offsets=tuple(offset for _, _, offset in chunks),
            chain=chain,
            back=back,
        )
        tiles.append(tile)
        tables.append(table)
        chain[:] = passed
        return chain[0]

    def far_job():
        tile, at, sums, mass = build([to_group(far_both[0], 1)], weights[:1], slots=sb)
        far_parts.extend((tile, at, mass, to_group(sums, -1)))
        return sums

    jobs = [
        (0, lambda: target_job(in_hbm(target_emb)[0])),
        (0, lambda: target_job(sibling_emb)),
        (0, lambda: near_job([(upper, lower, 0)])),
    ]

    def behind_job(step, *halves):
        if jobs and jobs[0][0] <= max(0, step - 2):
            halves = lax.optimization_barrier((halves, jobs.pop(0)[1]()))[0]
        return halves

    up_a, up_b, down_a, down_b = upper, lower, upper, lower
    for step in range(1, steps + 1):
        if step > 1:
            up_a, down_b = behind_job(step, up_a, down_b)
        up_a, down_b = around(up_a, 1), around(down_b, -1)
        if step < steps:
            up_b, down_a = behind_job(step, up_b, down_a)
            up_b, down_a = around(up_b, 1), around(down_a, -1)
            chunks = [(up_a, up_b, -step), (down_a, down_b, step)]
            jobs.append((step, functools.partial(near_job, chunks)))
        if step == 1:
            far_both[0] = lax.optimization_barrier((both, up_a))[0]
    far_job()
    for _, job in jobs:
        job()
    far_tiles, far_at, far_mass, from_far = far_parts
    near_job([(up_a, down_b, steps)], from_far)
    near_rows, all_mass = chain

    for sweep in range(ITERS):
        if sweep > 0:
            far_rows = far_row_sums(far_at, mine, theirs, target_mass, far_tiles)
            back = to_group(far_rows, -1)
            near_rows = row_sums(tables, mine, theirs, target_mass, sibling_mass, tiles, chips * sb)
            near_rows = add_own(me, near_rows, back)
        bit = 2
        while 2 * bit < dev_count:
            near_rows = near_rows + across(near_rows, bit)
            bit *= 2
        near_rows, own_rows = add_last(me, near_rows, across(near_rows, bit), sb)
        far_rows = to_group(own_rows, 1)
        mine = column_sums(tables, near_rows, all_mass, tiles, 2 * tb)
        mine = far_column_sums(far_at, mine, far_rows, far_mass, far_tiles)
        theirs = across(mine, 1)
    return scales(own_rows, source_mass, mine, theirs, target_mass)


def solution(mesh):
    placed = (
        P(("group", "dev"), None, None),
        P(("group", "dev"), None, None),
        P(("group", "dev"), None),
        P(("group", "dev"), None),
        P(("group", "dev"), None),
        P(("group", "dev"), None),
    )
    return jax.shard_map(
        local,
        mesh=mesh,
        in_specs=placed,
        out_specs=(P(("group", "dev"), None), P(("group", "dev"), None)),
        check_vma=False,
    )
```

```python
import functools
import math

import jax
import jax.numpy as jnp
from jax import lax
from jax.experimental import pallas as pl
from jax.experimental.pallas import tpu as pltpu
from jax.sharding import PartitionSpec as P

ITERS = 2

entropic_regularizer = 0.1
dustbin = 0.5
epsilon = 1e-06

VMEM = pl.BlockSpec(memory_space=pltpu.VMEM)
SMEM = pl.BlockSpec(memory_space=pltpu.SMEM)
HBM = pl.BlockSpec(memory_space=pltpu.HBM)
LIGHT = pl.CostEstimate(flops=1, bytes_accessed=1, transcendentals=0)
NT = (((1,), (1,)), ((), ()))
NN = (((1,), (0,)), ((), ()))


def in_vmem(*arrays):
    return [pltpu.with_memory_space_constraint(x, pltpu.VMEM) for x in arrays]


def in_smem(*arrays):
    return [pltpu.with_memory_space_constraint(x, pltpu.SMEM) for x in arrays]


def in_hbm(*arrays):
    return [pltpu.with_memory_space_constraint(x, pltpu.HBM) for x in arrays]


def split2(x):
    high = x.astype(jnp.bfloat16)
    low = (x - high.astype(jnp.float32)).astype(jnp.bfloat16)
    return high, low


def unit(x):
    return x * lax.rsqrt(jnp.mean(x * x, axis=-1, keepdims=True) + epsilon)


def stacked_parts(row):
    x = jnp.broadcast_to(row, (8, row.shape[1]))
    high = x.astype(jnp.bfloat16).astype(jnp.float32)
    rest = x - high
    low = rest.astype(jnp.bfloat16).astype(jnp.float32)
    place = lax.broadcasted_iota(jnp.int32, x.shape, 0)
    parts = jnp.where(place == 0, high, jnp.where(place == 1, low, jnp.where(place == 2, rest - low, 0.0)))
    return parts.astype(jnp.bfloat16)


def column_product(parts, tile):
    both = lax.dot_general(parts, tile, NN, preferred_element_type=jnp.float32)
    width = tile.shape[1] // 2
    return both[:, :width] + both[:, width:]


def row_product(parts, tile):
    return lax.dot_general(
        jnp.concatenate([parts, parts], axis=1), tile, NT, preferred_element_type=jnp.float32
    )


def target_kernel(emb_ref, out_ref, staged, arrived):
    parts = arrived.shape[0]
    share = emb_ref.shape[0] // parts
    copies = []
    for part in range(parts):
        spots = pl.ds(part * share, share)
        copies.append(pltpu.make_async_copy(emb_ref.at[spots], staged.at[spots], arrived.at[part]))
        copies[-1].start()

    def one(block, carry):
        high, low = split2(unit(staged[block]).T)
        out_ref[block] = jnp.concatenate([high, low], axis=1)
        return carry

    for part in range(parts):
        copies[part].wait()
        lax.fori_loop(part * share, (part + 1) * share, one, 0, unroll=4)


def target_operand(emb):
    blocks, rows, width = emb.shape
    parts = math.gcd(blocks, 8)
    return pl.pallas_call(
        target_kernel,
        out_shape=pltpu.VMEM((blocks, width, 2 * rows), jnp.bfloat16),
        in_specs=[pl.BlockSpec(memory_space=pl.ANY)],
        out_specs=VMEM,
        scratch_shapes=[pltpu.VMEM(emb.shape, jnp.float32), pltpu.SemaphoreType.DMA((parts,))],
        cost_estimate=LIGHT,
        compiler_params=pltpu.CompilerParams(vmem_limit_bytes=16 << 20),
        name="target_operand",
    )(emb)


def pack_kernel(device, emb, mass, cand_device, cand_block, upper, lower, both, named, blocks, arrived):
    sb, rows, width = emb.shape
    half, near = rows // 2, cand_device.shape[1]
    copies = [
        pltpu.make_async_copy(cand_device, named, arrived.at[0]),
        pltpu.make_async_copy(cand_block, blocks, arrived.at[1]),
        pltpu.make_async_copy(mass, lower.at[pl.ds(sb * half, sb)], arrived.at[2]),
    ]
    for block in range(sb):
        into = pl.ds(block * half, half)
        copies.append(pltpu.make_async_copy(emb.at[block, pl.ds(0, half)], upper.at[into], arrived.at[3 + 2 * block]))
        copies.append(
            pltpu.make_async_copy(emb.at[block, pl.ds(half, half)], lower.at[into], arrived.at[4 + 2 * block])
        )
    for copy in copies:
        copy.start()
    for copy in copies[:2]:
        copy.wait()
    upper[sb * half :] = jnp.zeros((sb, width), jnp.float32)
    upper[sb * half :, 0:near] = named[...].astype(jnp.float32)
    upper[sb * half :, near : near + blocks.shape[1]] = blocks[...].astype(jnp.float32)
    for copy in copies[2:]:
        copy.wait()
    count = upper.shape[0]
    both[0:count] = upper[...]
    both[count:] = lower[...]


def pack(device, emb, mass, cand_device, cand_block):
    sb, rows, width = emb.shape
    count = sb * (rows // 2 + 1)
    shape = pltpu.VMEM((count, width), jnp.float32)
    return pl.pallas_call(
        pack_kernel,
        out_shape=(shape, shape, pltpu.VMEM((2 * count, width), jnp.float32)),
        in_specs=[SMEM] + [HBM] * 4,
        out_specs=(VMEM, VMEM, VMEM),
        scratch_shapes=[
            pltpu.VMEM(cand_device.shape, jnp.int32),
            pltpu.VMEM(cand_block.shape, jnp.int32),
            pltpu.SemaphoreType.DMA((3 + 2 * sb,)),
        ],
        compiler_params=pltpu.CompilerParams(vmem_limit_bytes=16 << 20),
        name="pack",
    )(device, *in_hbm(emb, mass, cand_device, cand_block))


def chip_at(chips, chip, offset):
    odd = lax.rem(chip, 2)
    spot = jnp.where(odd == 1, chips - 1 - chip // 2, chip // 2) + offset
    spot = jnp.where(spot < 0, spot + chips, jnp.where(spot >= chips, spot - chips, spot))
    return jnp.where(spot < chips // 2, 2 * spot, 2 * chips - 1 - 2 * spot)


def tile_kernel(plan, *refs):
    chunks, slots, sb, half, tb, near, offsets, far, chained, closing = plan
    sides = 1 if far else 2
    refs = list(refs)
    device = refs.pop(0)
    if far:
        both = refs.pop(0)
        source = [both.at[pl.ds(start, sb * (half + 1))] for start in (0, sb * (half + 1))]
    else:
        source = [refs.pop(0) for _ in range(2 * chunks)]
    weight = [refs.pop(0) for _ in range(sides)]
    rows_in, mass_in = (refs.pop(0), refs.pop(0)) if chained else (None, None)
    back = refs.pop(0) if closing else None
    tiles, table, rows_out, mass_out, partial, units, staged, named, listed, arrived = refs
    count = chunks * sides * slots
    width = source[0].shape[1]
    scale = 1.0 / (width * entropic_regularizer)
    me = device[0]
    chips = rows_out.shape[0] // sb

    for chunk in range(chunks):
        staged[chunk * sb : (chunk + 1) * sb] = source[2 * chunk][sb * half :].astype(jnp.int32)
    copy = pltpu.make_async_copy(staged, named, arrived)
    copy.start()
    if chained:
        rows_out[...] = rows_in[...]
        mass_out[...] = mass_in[...]
    partial[...] = jnp.zeros_like(partial)
    place = lax.broadcasted_iota(jnp.int32, (8, 2 * width), 0)
    ones = jnp.where(place == 0, 1.0, 0.0).astype(jnp.bfloat16)
    for chunk in range(chunks):
        for block in range(sb):
            rows = pl.ds(block * half, half)
            left = jnp.concatenate([source[2 * chunk][rows], source[2 * chunk + 1][rows]], axis=0)
            units[chunk * sb + block] = jnp.concatenate(split2(unit(left)), axis=1)
    copy.wait()

    chip_of = []
    for chunk in range(chunks):
        at_chip = jnp.int32(0) if far else chip_at(chips, me // 2, offsets[chunk])
        chip_of.append(at_chip)
        for side in range(sides):
            base = (chunk * sides + side) * slots
            if far:
                for j in range(sb):
                    listed[base + j] = j
                    table[j] = named[j, 2 * near]
                continue
            wanted = me if side == 0 else me + 1 - 2 * lax.rem(me, 2)
            filled = jnp.int32(0)
            for block in range(sb):
                found, which = jnp.int32(0), jnp.int32(0)
                for k in range(near):
                    hit = named[chunk * sb + block, k] == wanted
                    found = jnp.where(hit, 1, found)
                    which = jnp.where(hit, named[chunk * sb + block, near + k], which)
                listed[base + filled] = block
                table[count + base + filled] = which
                filled = filled + found
            for j in range(slots):
                valid = j < filled
                block = jnp.where(valid, listed[base + j], sb)
                which = jnp.where(valid, table[count + base + j], 2 * tb)
                listed[base + j] = block
                table[base + j] = jnp.where(valid, at_chip * sb + block, chips * sb)
                table[count + base + j] = jnp.where(valid, which + side * tb, 2 * tb)

    for chunk in range(chunks):
        lower = source[2 * chunk + 1]
        for side in range(sides):
            for j in range(slots):
                at = (chunk * sides + side) * slots + j
                block = listed[at]
                right = weight[side][table[at] if far else lax.rem(table[count + at], tb)]
                both = lax.dot_general(
                    units[chunk * sb + lax.rem(block, sb)],
                    jnp.concatenate([right, right], axis=0),
                    NN,
                    preferred_element_type=jnp.float32,
                )
                nodes = both.shape[1] // 2
                affinity = both[:, :nodes] + both[:, nodes:]
                tile = jnp.exp(affinity * scale) * (1.0 / (8.0 * nodes))
                tile = jnp.concatenate(split2(tile), axis=1)
                tiles[at] = tile
                spot = chunk * (sb + 1) + block
                partial[spot] += lax.dot_general(ones, tile, NT, preferred_element_type=jnp.float32)
        start = pl.multiple_of(chip_of[chunk] * sb, sb)
        for block in range(sb):
            rows_out[pl.ds(start + block, 1)] = partial[chunk * (sb + 1) + block][0:1]
        mass_out[pl.ds(start, sb)] = lower[sb * half :]
    if closing:
        start = pl.multiple_of(me // 2 * sb, sb)
        rows_out[pl.ds(start, sb)] += back[...]


def build_tiles(device, source, weight, slots, sb, near, chips, offsets=(), chain=(), back=None):
    chunks, sides, far = max(1, len(source) // 2), len(weight), not offsets
    half, width = source[0].shape[0] // (sb * (1 + far)) - 1, source[0].shape[1]
    tb, nodes = weight[0].shape[0], weight[0].shape[2] // 2
    count = chunks * sides * slots
    plan = (chunks, slots, sb, half, tb, near, offsets, far, bool(chain), back is not None)
    operands = [device, *source, *in_vmem(*weight), *chain] + ([] if back is None else [back])
    rows = jax.ShapeDtypeStruct(((1 if far else chips) * sb, 2 * half), jnp.float32)
    return pl.pallas_call(
        functools.partial(tile_kernel, plan),
        out_shape=(
            pltpu.VMEM((count, 2 * half, 2 * nodes), jnp.bfloat16),
            pltpu.SMEM((count if far else 2 * count + 1,), jnp.int32),
            rows,
            rows,
        ),
        in_specs=[SMEM] + [VMEM] * (len(operands) - 1),
        out_specs=(VMEM, SMEM, VMEM, VMEM),
        scratch_shapes=[
            pltpu.VMEM((chunks * (sb + 1), 8, 2 * half), jnp.float32),
            pltpu.VMEM((chunks * sb, 2 * half, 2 * width), jnp.bfloat16),
            pltpu.VMEM((chunks * sb, width), jnp.int32),
            pltpu.SMEM((chunks * sb, width), jnp.int32),
            pltpu.SMEM((count + 1,), jnp.int32),
            pltpu.SemaphoreType.DMA,
        ],
        cost_estimate=LIGHT,
        compiler_params=pltpu.CompilerParams(vmem_limit_bytes=16 << 20),
        name="build_tiles",
    )(*operands)


SMALL = pltpu.CompilerParams(vmem_limit_bytes=16 << 20)


def add_kernel(device, *refs):
    parts, total, own = refs[:-2], refs[-2], refs[-1]
    sb = own.shape[0]
    total[...] = sum([part[...] for part in parts[1:]], parts[0][...])
    own[...] = total[pl.ds(pl.multiple_of(device[0] // 2 * sb, sb), sb)]


def add_last(device, parts, sb):
    return pl.pallas_call(
        add_kernel,
        out_shape=(
            jax.ShapeDtypeStruct(parts[0].shape, jnp.float32),
            jax.ShapeDtypeStruct((sb, parts[0].shape[1]), jnp.float32),
        ),
        in_specs=[SMEM] + [VMEM] * len(parts),
        out_specs=(VMEM, VMEM),
        compiler_params=SMALL,
        name="add_last",
    )(device, *parts)


def insert_kernel(device, rows, part, out):
    out[...] = rows[...]
    out[pl.ds(pl.multiple_of(device[0] // 2 * part.shape[0], part.shape[0]), part.shape[0])] += part[...]


def add_own(device, rows, part):
    return pl.pallas_call(
        insert_kernel,
        out_shape=jax.ShapeDtypeStruct(rows.shape, jnp.float32),
        in_specs=[SMEM, VMEM, VMEM],
        out_specs=VMEM,
        compiler_params=SMALL,
        name="add_own",
    )(device, rows, part)


def column_kernel(counts, *refs):
    refs = list(refs)
    tables = [refs.pop(0) for _ in counts]
    rows, mass = refs.pop(0), refs.pop(0)
    tiles = [refs.pop(0) for _ in counts]
    out, scale, total = refs
    count = rows.shape[0]
    scale[0:count] = mass[...] / (dustbin + rows[...])
    scale[count:] = jnp.zeros((8, scale.shape[1]), jnp.float32)
    total[...] = jnp.zeros_like(total)
    for part, slots in enumerate(counts):
        for slot in range(slots):
            parts = stacked_parts(scale[pl.ds(tables[part][slot], 1), :])
            total[tables[part][slots + slot]] += column_product(parts, tiles[part][slot])
    for block in range(out.shape[0]):
        out[block : block + 1] = jnp.sum(total[block], axis=0, keepdims=True)


def column_sums(tables, rows, mass, tiles, targets):
    counts = tuple(t.shape[0] for t in tiles)
    width, nodes = rows.shape[1], tiles[0].shape[2] // 2
    return pl.pallas_call(
        functools.partial(column_kernel, counts),
        out_shape=jax.ShapeDtypeStruct((targets, nodes), jnp.float32),
        in_specs=[SMEM] * len(tables) + [VMEM] * (2 + len(tiles)),
        out_specs=VMEM,
        scratch_shapes=[
            pltpu.VMEM((rows.shape[0] + 8, width), jnp.float32),
            pltpu.VMEM((targets + 1, 8, nodes), jnp.float32),
        ],
        cost_estimate=LIGHT,
        compiler_params=SMALL,
        name="column_sums",
    )(*in_smem(*tables), rows, mass, *in_vmem(*tiles))


def far_column_kernel(far_at, sums, far_rows, far_mass, tiles, out, scale):
    far = tiles.shape[0]
    out[...] = sums[...]
    scale[...] = far_mass[...] / (dustbin + far_rows[...])
    for slot in range(far):
        product = column_product(stacked_parts(scale[slot : slot + 1, :]), tiles[slot])
        out[pl.ds(far_at[slot], 1)] += jnp.sum(product, axis=0, keepdims=True)


def far_column_sums(far_at, sums, far_rows, far_mass, tiles):
    return pl.pallas_call(
        far_column_kernel,
        out_shape=jax.ShapeDtypeStruct(sums.shape, jnp.float32),
        in_specs=[SMEM] + [VMEM] * 4,
        out_specs=VMEM,
        scratch_shapes=[pltpu.VMEM(far_mass.shape, jnp.float32)],
        cost_estimate=LIGHT,
        compiler_params=SMALL,
        name="far_column_sums",
    )(*in_smem(far_at), sums, far_rows, far_mass, *in_vmem(tiles))


def scale_kernel(rows, mass, mine, theirs, target_mass, src, tgt):
    blocks = tgt.shape[0]
    src[...] = mass[...] / (dustbin + rows[...])
    tgt[...] = target_mass[...] / (dustbin + mine[0:blocks] + theirs[blocks : 2 * blocks])


def scales(rows, mass, mine, theirs, target_mass):
    return pl.pallas_call(
        scale_kernel,
        out_shape=(
            jax.ShapeDtypeStruct(mass.shape, jnp.float32),
            jax.ShapeDtypeStruct(target_mass.shape, jnp.float32),
        ),
        in_specs=[VMEM] * 5,
        out_specs=(VMEM, VMEM),
        compiler_params=SMALL,
        name="scales",
    )(rows, mass, mine, theirs, target_mass)


def far_row_kernel(far_at, mine, theirs, mass, tiles, out, scale):
    blocks = mass.shape[0]
    scale[...] = mass[...] / (dustbin + mine[0:blocks] + theirs[blocks : 2 * blocks])
    for slot in range(tiles.shape[0]):
        product = row_product(stacked_parts(scale[pl.ds(far_at[slot], 1), :]), tiles[slot])
        out[slot : slot + 1] = jnp.sum(product, axis=0, keepdims=True)


def far_row_sums(far_at, mine, theirs, mass, tiles):
    return pl.pallas_call(
        far_row_kernel,
        out_shape=jax.ShapeDtypeStruct(tiles.shape[:2], jnp.float32),
        in_specs=[SMEM] + [VMEM] * 4,
        out_specs=VMEM,
        scratch_shapes=[pltpu.VMEM(mass.shape, jnp.float32)],
        cost_estimate=LIGHT,
        compiler_params=SMALL,
        name="far_row_sums",
    )(*in_smem(far_at), mine, theirs, mass, *in_vmem(tiles))


def row_kernel(counts, *refs):
    refs = list(refs)
    tables = [refs.pop(0) for _ in counts]
    mine, theirs, mass, other_mass = [refs.pop(0) for _ in range(4)]
    tiles = [refs.pop(0) for _ in counts]
    out, scale, total = refs
    blocks = mass.shape[0]
    scale[0:blocks] = mass[...] / (dustbin + mine[0:blocks] + theirs[blocks : 2 * blocks])
    scale[blocks : 2 * blocks] = other_mass[...] / (dustbin + mine[blocks : 2 * blocks] + theirs[0:blocks])
    scale[2 * blocks :] = jnp.zeros((8, scale.shape[1]), jnp.float32)
    total[...] = jnp.zeros_like(total)
    for part, slots in enumerate(counts):
        for slot in range(slots):
            parts = stacked_parts(scale[pl.ds(tables[part][slots + slot], 1), :])
            total[tables[part][slot]] += row_product(parts, tiles[part][slot])
    for block in range(out.shape[0]):
        out[block : block + 1] = jnp.sum(total[block], axis=0, keepdims=True)


def row_sums(tables, mine, theirs, mass, other_mass, tiles, sources):
    counts = tuple(t.shape[0] for t in tiles)
    width, nodes = tiles[0].shape[1], tiles[0].shape[2] // 2
    return pl.pallas_call(
        functools.partial(row_kernel, counts),
        out_shape=jax.ShapeDtypeStruct((sources, width), jnp.float32),
        in_specs=[SMEM] * len(tables) + [VMEM] * (4 + len(tiles)),
        out_specs=VMEM,
        scratch_shapes=[
            pltpu.VMEM((mine.shape[0] + 8, nodes), jnp.float32),
            pltpu.VMEM((sources + 1, 8, width), jnp.float32),
        ],
        cost_estimate=LIGHT,
        compiler_params=SMALL,
        name="row_sums",
    )(*in_smem(*tables), mine, theirs, mass, other_mass, *in_vmem(*tiles))


def local(source_emb, target_emb, source_mass, target_mass, cand_device, cand_block):
    dev_count = lax.axis_size("dev")
    group_count = lax.axis_size("group")
    chips = dev_count // 2
    sb, tb = source_emb.shape[0], target_emb.shape[0]
    near = cand_device.shape[1]
    slot_cap = (near * sb + dev_count - 1) // dev_count + 1
    steps = chips // 2
    ring = list(range(0, chips, 2)) + list(range(chips - 1, 0, -2))

    def around(x, by):
        pairs = [
            (2 * ring[i] + core, 2 * ring[(i + by) % chips] + core) for i in range(chips) for core in range(2)
        ]
        return lax.ppermute(x, "dev", pairs)

    def across(x, bit):
        return lax.ppermute(x, "dev", [(i, i ^ bit) for i in range(dev_count)])

    def to_group(x, by):
        return lax.ppermute(x, "group", [(g, (g + by) % group_count) for g in range(group_count)])

    device = lax.axis_index("dev").astype(jnp.int32)
    me = device.reshape(1)

    upper, lower, both = pack(me, source_emb, source_mass, cand_device, cand_block)
    sibling_emb, sibling_mass = across(target_emb, 1), across(target_mass, 1)
    far_both = [both]

    weights, tiles, tables, chain, far_parts = [], [], [], [], []
    build = functools.partial(build_tiles, me, sb=sb, near=near, chips=chips)

    def target_job(emb):
        weights.append(target_operand(emb))
        return weights[-1]

    def near_job(chunks, back=None):
        tile, table, *passed = build(
            [x for up, low, _ in chunks for x in (up, low)],
            weights,
            slots=slot_cap,
            offsets=tuple(offset for _, _, offset in chunks),
            chain=chain,
            back=back,
        )
        tiles.append(tile)
        tables.append(table)
        chain[:] = passed
        return chain[0]

    def far_job():
        tile, at, sums, mass = build([to_group(far_both[0], 1)], weights[:1], slots=sb)
        far_parts.extend((tile, at, mass, to_group(sums, -1)))
        return sums

    jobs = [
        (0, lambda: target_job(in_hbm(target_emb)[0])),
        (0, lambda: target_job(sibling_emb)),
        (0, lambda: near_job([(upper, lower, 0)])),
    ]

    def behind_job(step, *halves):
        if jobs and jobs[0][0] <= max(0, step - 2):
            halves = lax.optimization_barrier((halves, jobs.pop(0)[1](), sibling_mass))[0]
        return halves

    up_a, up_b, down_a, down_b = upper, lower, upper, lower
    for step in range(1, steps + 1):
        if step > 1:
            up_a, down_b = behind_job(step, up_a, down_b)
        up_a, down_b = around(up_a, 1), around(down_b, -1)
        if step < steps:
            up_b, down_a = behind_job(step, up_b, down_a)
            up_b, down_a = around(up_b, 1), around(down_a, -1)
            chunks = [(up_a, up_b, -step), (down_a, down_b, step)]
            jobs.append((step, functools.partial(near_job, chunks)))
        if step == 1:
            far_both[0] = lax.optimization_barrier((both, up_a))[0]
    far_job()
    for _, job in jobs:
        job()
    far_tiles, far_at, far_mass, from_far = far_parts
    near_job([(up_a, down_b, steps)], from_far)
    near_rows, all_mass = chain

    for sweep in range(ITERS):
        if sweep > 0:
            far_rows = far_row_sums(far_at, mine, theirs, target_mass, far_tiles)
            back = to_group(far_rows, -1)
            near_rows = row_sums(tables, mine, theirs, target_mass, sibling_mass, tiles, chips * sb)
            near_rows = add_own(me, near_rows, back)
        bits = [1 << k for k in range(1, dev_count.bit_length() - 1)]
        parts = [near_rows]
        while bits:
            ways = [bits.pop() for _ in range(2 - len(bits) % 2)]
            ways = ways + [sum(ways)] if len(ways) == 2 else ways
            total = sum(parts[1:], parts[0])
            parts = [total] + [across(total, way) for way in ways]
        near_rows, own_rows = add_last(me, parts, sb)
        far_rows = to_group(own_rows, 1)
        mine = column_sums(tables, near_rows, all_mass, tiles, 2 * tb)
        mine = far_column_sums(far_at, mine, far_rows, far_mass, far_tiles)
        theirs = across(mine, 1)
    return scales(own_rows, source_mass, mine, theirs, target_mass)


def solution(mesh):
    placed = (
        P(("group", "dev"), None, None),
        P(("group", "dev"), None, None),
        P(("group", "dev"), None),
        P(("group", "dev"), None),
        P(("group", "dev"), None),
        P(("group", "dev"), None),
    )
    return jax.shard_map(
        local,
        mesh=mesh,
        in_specs=placed,
        out_specs=(P(("group", "dev"), None), P(("group", "dev"), None)),
        check_vma=False,
    )
```

```python
import functools
import math

import jax
import jax.numpy as jnp
from jax import lax
from jax.experimental import pallas as pl
from jax.experimental.pallas import tpu as pltpu
from jax.sharding import PartitionSpec as P

ITERS = 2

entropic_regularizer = 0.1
dustbin = 0.5
epsilon = 1e-06

VMEM = pl.BlockSpec(memory_space=pltpu.VMEM)
SMEM = pl.BlockSpec(memory_space=pltpu.SMEM)
HBM = pl.BlockSpec(memory_space=pltpu.HBM)
LIGHT = pl.CostEstimate(flops=1, bytes_accessed=1, transcendentals=0)
NT = (((1,), (1,)), ((), ()))
NN = (((1,), (0,)), ((), ()))


def in_vmem(*arrays):
    return [pltpu.with_memory_space_constraint(x, pltpu.VMEM) for x in arrays]


def in_smem(*arrays):
    return [pltpu.with_memory_space_constraint(x, pltpu.SMEM) for x in arrays]


def in_hbm(*arrays):
    return [pltpu.with_memory_space_constraint(x, pltpu.HBM) for x in arrays]


def split2(x):
    high = x.astype(jnp.bfloat16)
    low = (x - high.astype(jnp.float32)).astype(jnp.bfloat16)
    return high, low


def unit(x):
    return x * lax.rsqrt(jnp.mean(x * x, axis=-1, keepdims=True) + epsilon)


def stacked_parts(row):
    x = jnp.broadcast_to(row, (8, row.shape[1]))
    high = x.astype(jnp.bfloat16).astype(jnp.float32)
    rest = x - high
    low = rest.astype(jnp.bfloat16).astype(jnp.float32)
    place = lax.broadcasted_iota(jnp.int32, x.shape, 0)
    parts = jnp.where(place == 0, high, jnp.where(place == 1, low, jnp.where(place == 2, rest - low, 0.0)))
    return parts.astype(jnp.bfloat16)


def column_product(parts, tile):
    both = lax.dot_general(parts, tile, NN, preferred_element_type=jnp.float32)
    width = tile.shape[1] // 2
    return both[:, :width] + both[:, width:]


def row_product(parts, tile):
    return lax.dot_general(
        jnp.concatenate([parts, parts], axis=1), tile, NT, preferred_element_type=jnp.float32
    )


def target_kernel(emb_ref, out_ref, staged, arrived):
    parts = arrived.shape[0]
    share = emb_ref.shape[0] // parts
    copies = []
    for part in range(parts):
        spots = pl.ds(part * share, share)
        copies.append(pltpu.make_async_copy(emb_ref.at[spots], staged.at[spots], arrived.at[part]))
        copies[-1].start()

    def one(block, carry):
        high, low = split2(unit(staged[block]).T)
        out_ref[block] = jnp.concatenate([high, low], axis=1)
        return carry

    for part in range(parts):
        copies[part].wait()
        lax.fori_loop(part * share, (part + 1) * share, one, 0, unroll=4)


def target_operand(emb):
    blocks, rows, width = emb.shape
    parts = math.gcd(blocks, 8)
    return pl.pallas_call(
        target_kernel,
        out_shape=pltpu.VMEM((blocks, width, 2 * rows), jnp.bfloat16),
        in_specs=[pl.BlockSpec(memory_space=pl.ANY)],
        out_specs=VMEM,
        scratch_shapes=[pltpu.VMEM(emb.shape, jnp.float32), pltpu.SemaphoreType.DMA((parts,))],
        cost_estimate=LIGHT,
        compiler_params=pltpu.CompilerParams(vmem_limit_bytes=16 << 20),
        name="target_operand",
    )(emb)


def pack_kernel(device, emb, mass, cand_device, cand_block, upper, lower, both, named, blocks, arrived):
    sb, rows, width = emb.shape
    half, near = rows // 2, cand_device.shape[1]
    copies = [
        pltpu.make_async_copy(cand_device, named, arrived.at[0]),
        pltpu.make_async_copy(cand_block, blocks, arrived.at[1]),
        pltpu.make_async_copy(mass, lower.at[pl.ds(sb * half, sb)], arrived.at[2]),
    ]
    for block in range(sb):
        into = pl.ds(block * half, half)
        copies.append(pltpu.make_async_copy(emb.at[block, pl.ds(0, half)], upper.at[into], arrived.at[3 + 2 * block]))
        copies.append(
            pltpu.make_async_copy(emb.at[block, pl.ds(half, half)], lower.at[into], arrived.at[4 + 2 * block])
        )
    for copy in copies:
        copy.start()
    for copy in copies[:2]:
        copy.wait()
    upper[sb * half :] = jnp.zeros((sb, width), jnp.float32)
    upper[sb * half :, 0:near] = named[...].astype(jnp.float32)
    upper[sb * half :, near : near + blocks.shape[1]] = blocks[...].astype(jnp.float32)
    for copy in copies[2:]:
        copy.wait()
    count = upper.shape[0]
    both[0:count] = upper[...]
    both[count:] = lower[...]


def pack(device, emb, mass, cand_device, cand_block):
    sb, rows, width = emb.shape
    count = sb * (rows // 2 + 1)
    shape = pltpu.VMEM((count, width), jnp.float32)
    return pl.pallas_call(
        pack_kernel,
        out_shape=(shape, shape, pltpu.VMEM((2 * count, width), jnp.float32)),
        in_specs=[SMEM] + [HBM] * 4,
        out_specs=(VMEM, VMEM, VMEM),
        scratch_shapes=[
            pltpu.VMEM(cand_device.shape, jnp.int32),
            pltpu.VMEM(cand_block.shape, jnp.int32),
            pltpu.SemaphoreType.DMA((3 + 2 * sb,)),
        ],
        compiler_params=pltpu.CompilerParams(vmem_limit_bytes=16 << 20),
        name="pack",
    )(device, *in_hbm(emb, mass, cand_device, cand_block))


def chip_at(chips, chip, offset):
    odd = lax.rem(chip, 2)
    spot = jnp.where(odd == 1, chips - 1 - chip // 2, chip // 2) + offset
    spot = jnp.where(spot < 0, spot + chips, jnp.where(spot >= chips, spot - chips, spot))
    return jnp.where(spot < chips // 2, 2 * spot, 2 * chips - 1 - 2 * spot)


def tile_kernel(plan, *refs):
    chunks, slots, sb, half, tb, near, offsets, far, chained, closing, planned = plan
    sides = 1 if far else 2
    refs = list(refs)
    device = refs.pop(0)
    if far:
        both = refs.pop(0)
        source = [both.at[pl.ds(start, sb * (half + 1))] for start in (0, sb * (half + 1))]
    else:
        source = [refs.pop(0) for _ in range(2 * chunks)]
    weight = [refs.pop(0) for _ in range(sides)]
    rows_in, mass_in = (refs.pop(0), refs.pop(0)) if chained else (None, None)
    back = refs.pop(0) if closing else None
    if planned:
        table, listed, tiles, rows_out, mass_out, partial, units = refs
    else:
        tiles, table, rows_out, mass_out, partial, units, staged, named, listed, arrived = refs
    count = chunks * sides * slots
    width = source[0].shape[1]
    scale = 1.0 / (width * entropic_regularizer)
    me = device[0]
    chips = rows_out.shape[0] // sb

    if not planned:
        copy = fetch_named([source[2 * chunk] for chunk in range(chunks)], staged, named, arrived, sb, half)
    if chained:
        rows_out[...] = rows_in[...]
        mass_out[...] = mass_in[...]
    partial[...] = jnp.zeros_like(partial)
    place = lax.broadcasted_iota(jnp.int32, (8, 2 * width), 0)
    ones = jnp.where(place == 0, 1.0, 0.0).astype(jnp.bfloat16)
    for chunk in range(chunks):
        for block in range(sb):
            rows = pl.ds(block * half, half)
            left = jnp.concatenate([source[2 * chunk][rows], source[2 * chunk + 1][rows]], axis=0)
            units[chunk * sb + block] = jnp.concatenate(split2(unit(left)), axis=1)
    chip_of = [jnp.int32(0) if far else chip_at(chips, me // 2, offsets[chunk]) for chunk in range(chunks)]
    if not planned:
        copy.wait()
        for chunk in range(chunks):
            if far:
                for j in range(sb):
                    listed[j] = j
                    table[j] = named[j, 2 * near]
            else:
                list_slots(named, listed, table, me, chip_of[chunk], chunk, slots, sb, tb, near, chips, count)

    for chunk in range(chunks):
        lower = source[2 * chunk + 1]
        for side in range(sides):
            for j in range(slots):
                at = (chunk * sides + side) * slots + j
                block = listed[at]
                right = weight[side][table[at] if far else lax.rem(table[count + at], tb)]
                both = lax.dot_general(
                    units[chunk * sb + lax.rem(block, sb)],
                    jnp.concatenate([right, right], axis=0),
                    NN,
                    preferred_element_type=jnp.float32,
                )
                nodes = both.shape[1] // 2
                affinity = both[:, :nodes] + both[:, nodes:]
                tile = jnp.exp(affinity * scale) * (1.0 / (8.0 * nodes))
                tile = jnp.concatenate(split2(tile), axis=1)
                tiles[at] = tile
                spot = chunk * (sb + 1) + block
                partial[spot] += lax.dot_general(ones, tile, NT, preferred_element_type=jnp.float32)
        start = pl.multiple_of(chip_of[chunk] * sb, sb)
        for block in range(sb):
            rows_out[pl.ds(start + block, 1)] = partial[chunk * (sb + 1) + block][0:1]
        mass_out[pl.ds(start, sb)] = lower[sb * half :]
    if closing:
        start = pl.multiple_of(me // 2 * sb, sb)
        rows_out[pl.ds(start, sb)] += back[...]


def fetch_named(uppers, staged, named, arrived, sb, half):
    for chunk, upper in enumerate(uppers):
        staged[chunk * sb : (chunk + 1) * sb] = upper[sb * half :].astype(jnp.int32)
    copy = pltpu.make_async_copy(staged, named, arrived)
    copy.start()
    return copy


def list_slots(named, listed, table, me, at_chip, chunk, slots, sb, tb, near, chips, count):
    for side in range(2):
        base = (chunk * 2 + side) * slots
        wanted = me if side == 0 else me + 1 - 2 * lax.rem(me, 2)
        filled = jnp.int32(0)
        for block in range(sb):
            found, which = jnp.int32(0), jnp.int32(0)
            for k in range(near):
                hit = named[chunk * sb + block, k] == wanted
                found = jnp.where(hit, 1, found)
                which = jnp.where(hit, named[chunk * sb + block, near + k], which)
            listed[base + filled] = block
            table[count + base + filled] = which
            filled = filled + found
        for j in range(slots):
            valid = j < filled
            block = jnp.where(valid, listed[base + j], sb)
            which = jnp.where(valid, table[count + base + j], 2 * tb)
            listed[base + j] = block
            table[base + j] = jnp.where(valid, at_chip * sb + block, chips * sb)
            table[count + base + j] = jnp.where(valid, which + side * tb, 2 * tb)


def plan_kernel(plan, device, upper, table, listed, staged, named, arrived):
    slots, sb, half, tb, near, chips, offset = plan
    copy = fetch_named([upper], staged, named, arrived, sb, half)
    me = device[0]
    copy.wait()
    list_slots(
        named, listed, table, me, chip_at(chips, me // 2, offset), 0, slots, sb, tb, near, chips, 2 * slots
    )


def plan_tiles(device, upper, slots, sb, tb, near, chips, offset):
    half, width = upper.shape[0] // sb - 1, upper.shape[1]
    return pl.pallas_call(
        functools.partial(plan_kernel, (slots, sb, half, tb, near, chips, offset)),
        out_shape=(pltpu.SMEM((4 * slots + 1,), jnp.int32), pltpu.SMEM((2 * slots + 1,), jnp.int32)),
        in_specs=[SMEM, VMEM],
        out_specs=(SMEM, SMEM),
        scratch_shapes=[
            pltpu.VMEM((sb, width), jnp.int32),
            pltpu.SMEM((sb, width), jnp.int32),
            pltpu.SemaphoreType.DMA,
        ],
        cost_estimate=LIGHT,
        compiler_params=SMALL,
        name="plan_tiles",
    )(device, upper)


def build_tiles(device, source, weight, slots, sb, near, chips, offsets=(), chain=(), back=None, planned=()):
    chunks, sides, far = max(1, len(source) // 2), len(weight), not offsets
    half, width = source[0].shape[0] // (sb * (1 + far)) - 1, source[0].shape[1]
    tb, nodes = weight[0].shape[0], weight[0].shape[2] // 2
    count = chunks * sides * slots
    plan = (
        *(chunks, slots, sb, half, tb, near, offsets, far),
        *(bool(chain), back is not None, bool(planned)),
    )
    operands = [*source, *in_vmem(*weight), *chain] + ([] if back is None else [back])
    rows = jax.ShapeDtypeStruct(((1 if far else chips) * sb, 2 * half), jnp.float32)
    out_shape = [
        pltpu.VMEM((count, 2 * half, 2 * nodes), jnp.bfloat16),
        pltpu.SMEM((count if far else 2 * count + 1,), jnp.int32),
        rows,
        rows,
    ]
    out_specs = [VMEM, SMEM, VMEM, VMEM]
    scratch = [
        pltpu.VMEM((chunks * (sb + 1), 8, 2 * half), jnp.float32),
        pltpu.VMEM((chunks * sb, 2 * half, 2 * width), jnp.bfloat16),
        pltpu.VMEM((chunks * sb, width), jnp.int32),
        pltpu.SMEM((chunks * sb, width), jnp.int32),
        pltpu.SMEM((count + 1,), jnp.int32),
        pltpu.SemaphoreType.DMA,
    ]
    if planned:
        out_shape.pop(1)
        out_specs.pop(1)
        scratch = scratch[:2]
    out = pl.pallas_call(
        functools.partial(tile_kernel, plan),
        out_shape=out_shape,
        in_specs=[SMEM] + [VMEM] * len(operands) + [SMEM] * len(planned),
        out_specs=out_specs,
        scratch_shapes=scratch,
        cost_estimate=LIGHT,
        compiler_params=pltpu.CompilerParams(vmem_limit_bytes=16 << 20),
        name="build_tiles",
    )(device, *operands, *in_smem(*planned))
    return [out[0], planned[0], *out[1:]] if planned else out


SMALL = pltpu.CompilerParams(vmem_limit_bytes=16 << 20)


def add_kernel(*refs):
    parts, total = refs[:-1], refs[-1]
    total[...] = sum([part[...] for part in parts[1:]], parts[0][...])


def add_all(parts):
    return pl.pallas_call(
        add_kernel,
        out_shape=jax.ShapeDtypeStruct(parts[0].shape, jnp.float32),
        in_specs=[VMEM] * len(parts),
        out_specs=VMEM,
        compiler_params=SMALL,
        name="add_all",
    )(*parts)


def insert_kernel(device, rows, part, out):
    out[...] = rows[...]
    out[pl.ds(pl.multiple_of(device[0] // 2 * part.shape[0], part.shape[0]), part.shape[0])] += part[...]


def add_own(device, rows, part):
    return pl.pallas_call(
        insert_kernel,
        out_shape=jax.ShapeDtypeStruct(rows.shape, jnp.float32),
        in_specs=[SMEM, VMEM, VMEM],
        out_specs=VMEM,
        compiler_params=SMALL,
        name="add_own",
    )(device, rows, part)


def column_kernel(counts, *refs):
    refs = list(refs)
    tables = [refs.pop(0) for _ in counts]
    rows, mass = refs.pop(0), refs.pop(0)
    tiles = [refs.pop(0) for _ in counts]
    own, other, scale, total = refs
    count, blocks = rows.shape[0], own.shape[0]
    scale[0:count] = mass[...] / (dustbin + rows[...])
    scale[count:] = jnp.zeros((8, scale.shape[1]), jnp.float32)
    total[...] = jnp.zeros_like(total)
    for part, slots in enumerate(counts):
        for slot in range(slots):
            parts = stacked_parts(scale[pl.ds(tables[part][slot], 1), :])
            total[tables[part][slots + slot]] += column_product(parts, tiles[part][slot])
    for block in range(blocks):
        own[block : block + 1] = jnp.sum(total[block], axis=0, keepdims=True)
        other[block : block + 1] = jnp.sum(total[blocks + block], axis=0, keepdims=True)


def column_sums(tables, rows, mass, tiles, targets):
    counts = tuple(t.shape[0] for t in tiles)
    width, nodes = rows.shape[1], tiles[0].shape[2] // 2
    return pl.pallas_call(
        functools.partial(column_kernel, counts),
        out_shape=(jax.ShapeDtypeStruct((targets, nodes), jnp.float32),) * 2,
        in_specs=[SMEM] * len(tables) + [VMEM] * (2 + len(tiles)),
        out_specs=(VMEM, VMEM),
        scratch_shapes=[
            pltpu.VMEM((rows.shape[0] + 8, width), jnp.float32),
            pltpu.VMEM((2 * targets + 1, 8, nodes), jnp.float32),
        ],
        cost_estimate=LIGHT,
        compiler_params=SMALL,
        name="column_sums",
    )(*in_smem(*tables), rows, mass, *in_vmem(*tiles))


def closing_kernel(last, *refs):
    device, far_at, far_rows, far_mass, mine, theirs, target_mass, tiles = refs[:8]
    tgt, total = refs[-3], refs[-1]
    sb, slots = far_mass.shape[0], range(tiles.shape[0])
    start = pl.multiple_of(device[0] // 2 * sb, sb)
    scale = refs[-2]
    scale[...] = far_mass[...] / (dustbin + far_rows[pl.ds(start, sb)])
    total[...] = mine[...] + theirs[...]
    for slot in slots:
        product = column_product(stacked_parts(scale[slot : slot + 1, :]), tiles[slot])
        total[pl.ds(far_at[slot], 1)] += jnp.sum(product, axis=0, keepdims=True)
    tgt[...] = target_mass[...] / (dustbin + total[...])
    if last:
        rows, mass, src = refs[8:11]
        src[...] = mass[...] / (dustbin + rows[pl.ds(start, sb)])
    else:
        back = refs[8]
        for slot in slots:
            product = row_product(stacked_parts(tgt[pl.ds(far_at[slot], 1), :]), tiles[slot])
            back[slot : slot + 1] = jnp.sum(product, axis=0, keepdims=True)


def closing(device, far_at, far_rows, far_mass, mine, theirs, target_mass, tiles, rows=None, mass=None):
    last = mass is not None
    side = far_mass if mass is None else mass
    return pl.pallas_call(
        functools.partial(closing_kernel, last),
        out_shape=(
            jax.ShapeDtypeStruct(side.shape, jnp.float32),
            jax.ShapeDtypeStruct(target_mass.shape, jnp.float32),
        ),
        in_specs=[SMEM] * 2 + [VMEM] * (8 if last else 6),
        out_specs=(VMEM, VMEM),
        scratch_shapes=[pltpu.VMEM(far_mass.shape, jnp.float32), pltpu.VMEM(target_mass.shape, jnp.float32)],
        cost_estimate=LIGHT,
        compiler_params=SMALL,
        name="closing",
    )(
        *(device, *in_smem(far_at), far_rows, far_mass, mine, theirs, target_mass, *in_vmem(tiles)),
        *((rows, mass) if last else ()),
    )


def row_kernel(counts, *refs):
    refs = list(refs)
    tables = [refs.pop(0) for _ in counts]
    mine, theirs = refs.pop(0), refs.pop(0)
    tiles = [refs.pop(0) for _ in counts]
    out, scale, total = refs
    blocks = mine.shape[0]
    scale[0:blocks] = mine[...]
    scale[blocks : 2 * blocks] = theirs[...]
    scale[2 * blocks :] = jnp.zeros((8, scale.shape[1]), jnp.float32)
    total[...] = jnp.zeros_like(total)
    for part, slots in enumerate(counts):
        for slot in range(slots):
            parts = stacked_parts(scale[pl.ds(tables[part][slots + slot], 1), :])
            total[tables[part][slot]] += row_product(parts, tiles[part][slot])
    for block in range(out.shape[0]):
        out[block : block + 1] = jnp.sum(total[block], axis=0, keepdims=True)


def row_sums(tables, mine, theirs, tiles, sources):
    counts = tuple(t.shape[0] for t in tiles)
    width, nodes = tiles[0].shape[1], tiles[0].shape[2] // 2
    return pl.pallas_call(
        functools.partial(row_kernel, counts),
        out_shape=jax.ShapeDtypeStruct((sources, width), jnp.float32),
        in_specs=[SMEM] * len(tables) + [VMEM] * (2 + len(tiles)),
        out_specs=VMEM,
        scratch_shapes=[
            pltpu.VMEM((2 * mine.shape[0] + 8, nodes), jnp.float32),
            pltpu.VMEM((sources + 1, 8, width), jnp.float32),
        ],
        cost_estimate=LIGHT,
        compiler_params=SMALL,
        name="row_sums",
    )(*in_smem(*tables), mine, theirs, *in_vmem(*tiles))


def local(source_emb, target_emb, source_mass, target_mass, cand_device, cand_block):
    dev_count = lax.axis_size("dev")
    group_count = lax.axis_size("group")
    chips = dev_count // 2
    sb, tb = source_emb.shape[0], target_emb.shape[0]
    near = cand_device.shape[1]
    slot_cap = (near * sb + dev_count - 1) // dev_count + 1
    steps = chips // 2
    ring = list(range(0, chips, 2)) + list(range(chips - 1, 0, -2))

    def around(x, by):
        pairs = [
            (2 * ring[i] + core, 2 * ring[(i + by) % chips] + core) for i in range(chips) for core in range(2)
        ]
        return lax.ppermute(x, "dev", pairs)

    def across(x, bit):
        return lax.ppermute(x, "dev", [(i, i ^ bit) for i in range(dev_count)])

    def to_group(x, by):
        return lax.ppermute(x, "group", [(g, (g + by) % group_count) for g in range(group_count)])

    device = lax.axis_index("dev").astype(jnp.int32)
    me = device.reshape(1)

    upper, lower, both = pack(me, source_emb, source_mass, cand_device, cand_block)
    sibling_emb = across(target_emb, 1)
    far_both = [both]

    weights, tiles, tables, chain, far_parts = [], [], [], [], []
    build = functools.partial(build_tiles, me, sb=sb, near=near, chips=chips)

    def target_job(emb):
        weights.append(target_operand(emb))
        return weights[-1]

    def near_job(chunks, back=None, planned=()):
        tile, table, *passed = build(
            [x for up, low, _ in chunks for x in (up, low)],
            weights,
            slots=slot_cap,
            offsets=tuple(offset for _, _, offset in chunks),
            chain=chain,
            back=back,
            planned=planned,
        )
        tiles.append(tile)
        tables.append(table)
        chain[:] = passed
        return chain[0]

    def far_job():
        tile, at, sums, mass = build([to_group(far_both[0], 1)], weights[:1], slots=sb)
        far_parts.extend((tile, at, mass, to_group(sums, -1)))
        return sums

    jobs = [
        (0, lambda: target_job(in_hbm(target_emb)[0])),
        (0, lambda: target_job(sibling_emb)),
        (0, lambda: near_job([(upper, lower, 0)])),
    ]

    def behind_job(step, *halves):
        if jobs and jobs[0][0] <= max(0, step - 2):
            halves, _ = lax.optimization_barrier((halves, jobs.pop(0)[1]()))
        return halves

    up_a, up_b, down_a, down_b = upper, lower, upper, lower
    for step in range(1, steps + 1):
        if step > 1:
            up_a, down_b = behind_job(step, up_a, down_b)
        up_a, down_b = around(up_a, 1), around(down_b, -1)
        if step < steps:
            up_b, down_a = behind_job(step, up_b, down_a)
            up_b, down_a = around(up_b, 1), around(down_a, -1)
            chunks = [(up_a, up_b, -step), (down_a, down_b, step)]
            jobs.append((step, functools.partial(near_job, chunks)))
        if step == 1:
            far_both[0] = lax.optimization_barrier((both, up_a))[0]
    far_job()
    for _, job in jobs:
        job()
    far_tiles, far_at, far_mass, from_far = far_parts
    planned = plan_tiles(me, up_a, slot_cap, sb, target_emb.shape[0], near, chips, steps)
    near_job([(up_a, down_b, steps)], from_far, planned)
    near_rows, all_mass = chain

    for sweep in range(ITERS):
        if sweep > 0:
            back = to_group(extra, -1)
            near_rows = row_sums(tables, scale, across(scale, 1), tiles, chips * sb)
            near_rows = add_own(me, near_rows, back)
        bits = [1 << k for k in range(1, dev_count.bit_length() - 1)]
        parts = [near_rows]
        while bits:
            ways = [bits.pop() for _ in range(2 - len(bits) % 2)]
            ways = [sum(ways)] + ways if len(ways) == 2 else ways
            total = sum(parts[1:], parts[0])
            parts = [total] + [across(total, way) for way in ways]
        near_rows = add_all(parts)
        all_rows = to_group(near_rows, 1)
        mine, other = column_sums(tables, near_rows, all_mass, tiles, target_emb.shape[0])
        theirs = across(other, 1)
        own = (near_rows, source_mass) if sweep == ITERS - 1 else ()
        extra, scale = closing(
            me, far_at, all_rows, far_mass, mine, theirs, target_mass, far_tiles, *own
        )
    return (extra, scale)


def solution(mesh):
    placed = (
        P(("group", "dev"), None, None),
        P(("group", "dev"), None, None),
        P(("group", "dev"), None),
        P(("group", "dev"), None),
        P(("group", "dev"), None),
        P(("group", "dev"), None),
    )
    return jax.shard_map(
        local,
        mesh=mesh,
        in_specs=placed,
        out_specs=(P(("group", "dev"), None), P(("group", "dev"), None)),
        check_vma=False,
    )
```

```python
import functools
import math

import jax
import jax.numpy as jnp
from jax import lax
from jax.experimental import pallas as pl
from jax.experimental.pallas import tpu as pltpu
from jax.sharding import PartitionSpec as P

ITERS = 2

entropic_regularizer = 0.1
dustbin = 0.5
epsilon = 1e-06

VMEM = pl.BlockSpec(memory_space=pltpu.VMEM)
SMEM = pl.BlockSpec(memory_space=pltpu.SMEM)
HBM = pl.BlockSpec(memory_space=pltpu.HBM)
NT = (((1,), (1,)), ((), ()))
NN = (((1,), (0,)), ((), ()))


def in_vmem(*arrays):
    return [pltpu.with_memory_space_constraint(x, pltpu.VMEM) for x in arrays]


def in_smem(*arrays):
    return [pltpu.with_memory_space_constraint(x, pltpu.SMEM) for x in arrays]


def in_hbm(*arrays):
    return [pltpu.with_memory_space_constraint(x, pltpu.HBM) for x in arrays]


def split2(x):
    high = x.astype(jnp.bfloat16)
    low = (x - high.astype(jnp.float32)).astype(jnp.bfloat16)
    return high, low


def unit(x):
    return x * lax.rsqrt(jnp.mean(x * x, axis=-1, keepdims=True) + epsilon)


def stacked_parts(row):
    x = jnp.broadcast_to(row, (8, row.shape[1]))
    high = x.astype(jnp.bfloat16).astype(jnp.float32)
    rest = x - high
    low = rest.astype(jnp.bfloat16).astype(jnp.float32)
    place = lax.broadcasted_iota(jnp.int32, x.shape, 0)
    parts = jnp.where(place == 0, high, jnp.where(place == 1, low, jnp.where(place == 2, rest - low, 0.0)))
    return parts.astype(jnp.bfloat16)


def column_product(parts, tile):
    both = lax.dot_general(parts, tile, NN, preferred_element_type=jnp.float32)
    width = tile.shape[1] // 2
    return both[:, :width] + both[:, width:]


def row_product(parts, tile):
    return lax.dot_general(
        jnp.concatenate([parts, parts], axis=1), tile, NT, preferred_element_type=jnp.float32
    )


def target_kernel(emb_ref, out_ref, staged, arrived):
    parts = arrived.shape[0]
    share = emb_ref.shape[0] // parts
    copies = []
    for part in range(parts):
        spots = pl.ds(part * share, share)
        copies.append(pltpu.make_async_copy(emb_ref.at[spots], staged.at[spots], arrived.at[part]))
        copies[-1].start()

    def one(block, carry):
        high, low = split2(unit(staged[block]).T)
        out_ref[block] = jnp.concatenate([high, low], axis=1)
        return carry

    for part in range(parts):
        copies[part].wait()
        lax.fori_loop(part * share, (part + 1) * share, one, 0, unroll=4)


def target_operand(emb):
    blocks, rows, width = emb.shape
    parts = math.gcd(blocks, 8)
    return pl.pallas_call(
        target_kernel,
        out_shape=pltpu.VMEM((blocks, width, 2 * rows), jnp.bfloat16),
        in_specs=[pl.BlockSpec(memory_space=pl.ANY)],
        out_specs=VMEM,
        scratch_shapes=[pltpu.VMEM(emb.shape, jnp.float32), pltpu.SemaphoreType.DMA((parts,))],
        compiler_params=pltpu.CompilerParams(vmem_limit_bytes=16 << 20),
        name="target_operand",
    )(emb)


def pack_kernel(device, emb, mass, cand_device, cand_block, upper, lower, both, named, blocks, arrived):
    sb, rows, width = emb.shape
    half, near = rows // 2, cand_device.shape[1]
    copies = [
        pltpu.make_async_copy(cand_device, named, arrived.at[0]),
        pltpu.make_async_copy(cand_block, blocks, arrived.at[1]),
        pltpu.make_async_copy(mass, lower.at[pl.ds(sb * half, sb)], arrived.at[2]),
    ]
    for block in range(sb):
        into = pl.ds(block * half, half)
        copies.append(pltpu.make_async_copy(emb.at[block, pl.ds(0, half)], upper.at[into], arrived.at[3 + 2 * block]))
        copies.append(
            pltpu.make_async_copy(emb.at[block, pl.ds(half, half)], lower.at[into], arrived.at[4 + 2 * block])
        )
    for copy in copies:
        copy.start()
    for copy in copies[:2]:
        copy.wait()
    upper[sb * half :] = jnp.zeros((sb, width), jnp.float32)
    upper[sb * half :, 0:near] = named[...].astype(jnp.float32)
    upper[sb * half :, near : near + blocks.shape[1]] = blocks[...].astype(jnp.float32)
    for copy in copies[2:]:
        copy.wait()
    count = upper.shape[0]
    both[0:count] = upper[...]
    both[count:] = lower[...]


def pack(device, emb, mass, cand_device, cand_block):
    sb, rows, width = emb.shape
    count = sb * (rows // 2 + 1)
    shape = pltpu.VMEM((count, width), jnp.float32)
    return pl.pallas_call(
        pack_kernel,
        out_shape=(shape, shape, pltpu.VMEM((2 * count, width), jnp.float32)),
        in_specs=[SMEM] + [HBM] * 4,
        out_specs=(VMEM, VMEM, VMEM),
        scratch_shapes=[
            pltpu.VMEM(cand_device.shape, jnp.int32),
            pltpu.VMEM(cand_block.shape, jnp.int32),
            pltpu.SemaphoreType.DMA((3 + 2 * sb,)),
        ],
        compiler_params=pltpu.CompilerParams(vmem_limit_bytes=16 << 20),
        name="pack",
    )(device, *in_hbm(emb, mass, cand_device, cand_block))


def chip_at(chips, chip, offset):
    odd = lax.rem(chip, 2)
    spot = jnp.where(odd == 1, chips - 1 - chip // 2, chip // 2) + offset
    spot = jnp.where(spot < 0, spot + chips, jnp.where(spot >= chips, spot - chips, spot))
    return jnp.where(spot < chips // 2, 2 * spot, 2 * chips - 1 - 2 * spot)


def tile_kernel(plan, *refs):
    chunks, slots, sb, half, tb, near, offsets, far, chained, closing, planned = plan
    sides = 1 if far else 2
    refs = list(refs)
    device = refs.pop(0)
    if far:
        both = refs.pop(0)
        source = [both.at[pl.ds(start, sb * (half + 1))] for start in (0, sb * (half + 1))]
    else:
        source = [refs.pop(0) for _ in range(2 * chunks)]
    weight = [refs.pop(0) for _ in range(sides)]
    rows_in, mass_in = (refs.pop(0), refs.pop(0)) if chained else (None, None)
    back = refs.pop(0) if closing else None
    turned = None
    if planned:
        table, listed, tiles, rows_out, mass_out, partial, units = refs
    elif far:
        tiles, table, rows_out, mass_out, partial, units, staged, named, listed, arrived = refs
    else:
        tiles, table, rows_out, mass_out, turned, partial, units, staged, named, listed, arrived = refs
    count = chunks * sides * slots
    width = source[0].shape[1]
    scale = 1.0 / (width * entropic_regularizer)
    me = device[0]
    chips = rows_out.shape[0] // sb

    if not planned:
        copy = fetch_named([source[2 * chunk] for chunk in range(chunks)], staged, named, arrived, sb, half)
    if chained:
        rows_out[...] = rows_in[...]
        mass_out[...] = mass_in[...]
    partial[...] = jnp.zeros_like(partial)
    place = lax.broadcasted_iota(jnp.int32, (8, 2 * width), 0)
    ones = jnp.where(place == 0, 1.0, 0.0).astype(jnp.bfloat16)
    for chunk in range(chunks):
        for block in range(sb):
            rows = pl.ds(block * half, half)
            left = jnp.concatenate([source[2 * chunk][rows], source[2 * chunk + 1][rows]], axis=0)
            units[chunk * sb + block] = jnp.concatenate(split2(unit(left)), axis=1)
    chip_of = [jnp.int32(0) if far else chip_at(chips, me // 2, offsets[chunk]) for chunk in range(chunks)]
    if not planned:
        copy.wait()
        for chunk in range(chunks):
            if far:
                for j in range(sb):
                    listed[j] = j
                    table[j] = named[j, 2 * near]
            else:
                list_slots(named, listed, table, me, chip_of[chunk], chunk, slots, sb, tb, near, chips, count)

    for chunk in range(chunks):
        lower = source[2 * chunk + 1]
        for side in range(sides):
            for j in range(slots):
                at = (chunk * sides + side) * slots + j
                block = listed[at]
                right = weight[side][table[at] if far else lax.rem(table[count + at], tb)]
                both = lax.dot_general(
                    units[chunk * sb + lax.rem(block, sb)],
                    jnp.concatenate([right, right], axis=0),
                    NN,
                    preferred_element_type=jnp.float32,
                )
                nodes = both.shape[1] // 2
                affinity = both[:, :nodes] + both[:, nodes:]
                tile = jnp.exp(affinity * scale) * (1.0 / (8.0 * nodes))
                if turned is not None:
                    turned[at] = jnp.concatenate(split2(tile.T), axis=1)
                tile = jnp.concatenate(split2(tile), axis=1)
                tiles[at] = tile
                spot = chunk * (sb + 1) + block
                partial[spot] += lax.dot_general(ones, tile, NT, preferred_element_type=jnp.float32)
        start = pl.multiple_of(chip_of[chunk] * sb, sb)
        for block in range(sb):
            rows_out[pl.ds(start + block, 1)] = partial[chunk * (sb + 1) + block][0:1]
        mass_out[pl.ds(start, sb)] = lower[sb * half :]
    if closing:
        start = pl.multiple_of(me // 2 * sb, sb)
        rows_out[pl.ds(start, sb)] += back[...]


def fetch_named(uppers, staged, named, arrived, sb, half):
    for chunk, upper in enumerate(uppers):
        staged[chunk * sb : (chunk + 1) * sb] = upper[sb * half :].astype(jnp.int32)
    copy = pltpu.make_async_copy(staged, named, arrived)
    copy.start()
    return copy


def list_slots(named, listed, table, me, at_chip, chunk, slots, sb, tb, near, chips, count):
    for side in range(2):
        base = (chunk * 2 + side) * slots
        wanted = me if side == 0 else me + 1 - 2 * lax.rem(me, 2)
        filled = jnp.int32(0)
        for block in range(sb):
            found, which = jnp.int32(0), jnp.int32(0)
            for k in range(near):
                hit = named[chunk * sb + block, k] == wanted
                found = jnp.where(hit, 1, found)
                which = jnp.where(hit, named[chunk * sb + block, near + k], which)
            listed[base + filled] = block
            table[count + base + filled] = which
            filled = filled + found
        for j in range(slots):
            valid = j < filled
            block = jnp.where(valid, listed[base + j], sb)
            which = jnp.where(valid, table[count + base + j], 2 * tb)
            listed[base + j] = block
            table[base + j] = jnp.where(valid, at_chip * sb + block, chips * sb)
            table[count + base + j] = jnp.where(valid, which + side * tb, 2 * tb)


def plan_kernel(plan, device, upper, table, listed, staged, named, arrived):
    slots, sb, half, tb, near, chips, offset = plan
    copy = fetch_named([upper], staged, named, arrived, sb, half)
    me = device[0]
    copy.wait()
    list_slots(
        named, listed, table, me, chip_at(chips, me // 2, offset), 0, slots, sb, tb, near, chips, 2 * slots
    )


def plan_tiles(device, upper, slots, sb, tb, near, chips, offset):
    half, width = upper.shape[0] // sb - 1, upper.shape[1]
    return pl.pallas_call(
        functools.partial(plan_kernel, (slots, sb, half, tb, near, chips, offset)),
        out_shape=(pltpu.SMEM((4 * slots + 1,), jnp.int32), pltpu.SMEM((2 * slots + 1,), jnp.int32)),
        in_specs=[SMEM, VMEM],
        out_specs=(SMEM, SMEM),
        scratch_shapes=[
            pltpu.VMEM((sb, width), jnp.int32),
            pltpu.SMEM((sb, width), jnp.int32),
            pltpu.SemaphoreType.DMA,
        ],
        compiler_params=SMALL,
        name="plan_tiles",
    )(device, upper)


def build_tiles(device, source, weight, slots, sb, near, chips, offsets=(), chain=(), back=None, planned=()):
    chunks, sides, far = max(1, len(source) // 2), len(weight), not offsets
    half, width = source[0].shape[0] // (sb * (1 + far)) - 1, source[0].shape[1]
    tb, nodes = weight[0].shape[0], weight[0].shape[2] // 2
    count = chunks * sides * slots
    plan = (
        *(chunks, slots, sb, half, tb, near, offsets, far),
        *(bool(chain), back is not None, bool(planned)),
    )
    operands = [*source, *in_vmem(*weight), *chain] + ([] if back is None else [back])
    rows = jax.ShapeDtypeStruct(((1 if far else chips) * sb, 2 * half), jnp.float32)
    out_shape = [
        pltpu.VMEM((count, 2 * half, 2 * nodes), jnp.bfloat16),
        pltpu.SMEM((count if far else 2 * count + 1,), jnp.int32),
        rows,
        rows,
    ]
    out_specs = [VMEM, SMEM, VMEM, VMEM]
    if not far and not planned:
        out_shape.append(pltpu.VMEM((count, nodes, 4 * half), jnp.bfloat16))
        out_specs.append(VMEM)
    scratch = [
        pltpu.VMEM((chunks * (sb + 1), 8, 2 * half), jnp.float32),
        pltpu.VMEM((chunks * sb, 2 * half, 2 * width), jnp.bfloat16),
        pltpu.VMEM((chunks * sb, width), jnp.int32),
        pltpu.SMEM((chunks * sb, width), jnp.int32),
        pltpu.SMEM((count + 1,), jnp.int32),
        pltpu.SemaphoreType.DMA,
    ]
    if planned:
        out_shape.pop(1)
        out_specs.pop(1)
        scratch = scratch[:2]
    out = pl.pallas_call(
        functools.partial(tile_kernel, plan),
        out_shape=out_shape,
        in_specs=[SMEM] + [VMEM] * len(operands) + [SMEM] * len(planned),
        out_specs=out_specs,
        scratch_shapes=scratch,
        compiler_params=pltpu.CompilerParams(vmem_limit_bytes=16 << 20),
        name="build_tiles",
    )(device, *operands, *in_smem(*planned))
    return [out[0], planned[0], *out[1:]] if planned else out


SMALL = pltpu.CompilerParams(vmem_limit_bytes=16 << 20)


def add_kernel(*refs):
    parts, total = refs[:-1], refs[-1]
    total[...] = sum([part[...] for part in parts[1:]], parts[0][...])


def add_all(parts):
    return pl.pallas_call(
        add_kernel,
        out_shape=jax.ShapeDtypeStruct(parts[0].shape, jnp.float32),
        in_specs=[VMEM] * len(parts),
        out_specs=VMEM,
        compiler_params=SMALL,
        name="add_all",
    )(*parts)


def insert_kernel(device, rows, part, out):
    out[...] = rows[...]
    out[pl.ds(pl.multiple_of(device[0] // 2 * part.shape[0], part.shape[0]), part.shape[0])] += part[...]


def add_own(device, rows, part):
    return pl.pallas_call(
        insert_kernel,
        out_shape=jax.ShapeDtypeStruct(rows.shape, jnp.float32),
        in_specs=[SMEM, VMEM, VMEM],
        out_specs=VMEM,
        compiler_params=SMALL,
        name="add_own",
    )(device, rows, part)


def column_kernel(counts, *refs):
    refs = list(refs)
    tables = [refs.pop(0) for _ in counts]
    rows, mass = refs.pop(0), refs.pop(0)
    tiles = [refs.pop(0) for _ in counts]
    own, other, scale, total = refs
    count, blocks = rows.shape[0], own.shape[0]
    scale[0:count] = mass[...] / (dustbin + rows[...])
    scale[count:] = jnp.zeros((8, scale.shape[1]), jnp.float32)
    total[...] = jnp.zeros_like(total)
    for part, slots in enumerate(counts):
        for slot in range(slots):
            parts = stacked_parts(scale[pl.ds(tables[part][slot], 1), :])
            total[tables[part][slots + slot]] += column_product(parts, tiles[part][slot])
    for block in range(blocks):
        own[block : block + 1] = jnp.sum(total[block], axis=0, keepdims=True)
        other[block : block + 1] = jnp.sum(total[blocks + block], axis=0, keepdims=True)


def column_sums(tables, rows, mass, tiles, targets):
    counts = tuple(t.shape[0] for t in tiles)
    width, nodes = rows.shape[1], tiles[0].shape[2] // 2
    return pl.pallas_call(
        functools.partial(column_kernel, counts),
        out_shape=(jax.ShapeDtypeStruct((targets, nodes), jnp.float32),) * 2,
        in_specs=[SMEM] * len(tables) + [VMEM] * (2 + len(tiles)),
        out_specs=(VMEM, VMEM),
        scratch_shapes=[
            pltpu.VMEM((rows.shape[0] + 8, width), jnp.float32),
            pltpu.VMEM((2 * targets + 1, 8, nodes), jnp.float32),
        ],
        compiler_params=SMALL,
        name="column_sums",
    )(*in_smem(*tables), rows, mass, *in_vmem(*tiles))


def closing_kernel(last, *refs):
    device, far_at, far_rows, far_mass, mine, theirs, target_mass, tiles = refs[:8]
    tgt, total = refs[-3], refs[-1]
    sb, slots = far_mass.shape[0], range(tiles.shape[0])
    start = pl.multiple_of(device[0] // 2 * sb, sb)
    scale = refs[-2]
    scale[...] = far_mass[...] / (dustbin + far_rows[pl.ds(start, sb)])
    total[...] = mine[...] + theirs[...]
    for slot in slots:
        product = column_product(stacked_parts(scale[slot : slot + 1, :]), tiles[slot])
        total[pl.ds(far_at[slot], 1)] += jnp.sum(product, axis=0, keepdims=True)
    tgt[...] = target_mass[...] / (dustbin + total[...])
    if last:
        rows, mass, src = refs[8:11]
        src[...] = mass[...] / (dustbin + rows[pl.ds(start, sb)])
    else:
        back = refs[8]
        for slot in slots:
            product = row_product(stacked_parts(tgt[pl.ds(far_at[slot], 1), :]), tiles[slot])
            back[slot : slot + 1] = jnp.sum(product, axis=0, keepdims=True)


def closing(device, far_at, far_rows, far_mass, mine, theirs, target_mass, tiles, rows=None, mass=None):
    last = mass is not None
    side = far_mass if mass is None else mass
    return pl.pallas_call(
        functools.partial(closing_kernel, last),
        out_shape=(
            jax.ShapeDtypeStruct(side.shape, jnp.float32),
            jax.ShapeDtypeStruct(target_mass.shape, jnp.float32),
        ),
        in_specs=[SMEM] * 2 + [VMEM] * (8 if last else 6),
        out_specs=(VMEM, VMEM),
        scratch_shapes=[pltpu.VMEM(far_mass.shape, jnp.float32), pltpu.VMEM(target_mass.shape, jnp.float32)],
        compiler_params=SMALL,
        name="closing",
    )(
        *(device, *in_smem(far_at), far_rows, far_mass, mine, theirs, target_mass, *in_vmem(tiles)),
        *((rows, mass) if last else ()),
    )


def row_kernel(counts, *refs):
    refs = list(refs)
    tables = [refs.pop(0) for _ in counts]
    mine, theirs = refs.pop(0), refs.pop(0)
    tiles = [refs.pop(0) for _ in counts]
    out, scale, total = refs
    blocks = mine.shape[0]
    scale[0:blocks] = mine[...]
    scale[blocks : 2 * blocks] = theirs[...]
    scale[2 * blocks :] = jnp.zeros((8, scale.shape[1]), jnp.float32)
    total[...] = jnp.zeros_like(total)
    for part, slots in enumerate(counts):
        for slot in range(slots):
            parts = stacked_parts(scale[pl.ds(tables[part][slots + slot], 1), :])
            product = row_product if part == len(counts) - 1 else column_product
            total[tables[part][slot]] += product(parts, tiles[part][slot])
    for block in range(out.shape[0]):
        out[block : block + 1] = jnp.sum(total[block], axis=0, keepdims=True)


def row_sums(tables, mine, theirs, tiles, sources):
    counts = tuple(t.shape[0] for t in tiles)
    width, nodes = tiles[0].shape[1], tiles[0].shape[2] // 2
    return pl.pallas_call(
        functools.partial(row_kernel, counts),
        out_shape=jax.ShapeDtypeStruct((sources, width), jnp.float32),
        in_specs=[SMEM] * len(tables) + [VMEM] * (2 + len(tiles)),
        out_specs=VMEM,
        scratch_shapes=[
            pltpu.VMEM((2 * mine.shape[0] + 8, nodes), jnp.float32),
            pltpu.VMEM((sources + 1, 8, width), jnp.float32),
        ],
        compiler_params=SMALL,
        name="row_sums",
    )(*in_smem(*tables), mine, theirs, *in_vmem(*tiles))


def local(source_emb, target_emb, source_mass, target_mass, cand_device, cand_block):
    dev_count = lax.axis_size("dev")
    group_count = lax.axis_size("group")
    chips = dev_count // 2
    sb, tb = source_emb.shape[0], target_emb.shape[0]
    near = cand_device.shape[1]
    slot_cap = (near * sb + dev_count - 1) // dev_count + 1
    steps = chips // 2
    ring = list(range(0, chips, 2)) + list(range(chips - 1, 0, -2))

    def around(x, by):
        pairs = [
            (2 * ring[i] + core, 2 * ring[(i + by) % chips] + core) for i in range(chips) for core in range(2)
        ]
        return lax.ppermute(x, "dev", pairs)

    def across(x, bit):
        return lax.ppermute(x, "dev", [(i, i ^ bit) for i in range(dev_count)])

    def to_group(x, by):
        return lax.ppermute(x, "group", [(g, (g + by) % group_count) for g in range(group_count)])

    device = lax.axis_index("dev").astype(jnp.int32)
    me = device.reshape(1)

    upper, lower, both = pack(me, source_emb, source_mass, cand_device, cand_block)
    sibling_emb = across(target_emb, 1)
    far_both = [both]

    weights, tiles, row_tiles, tables, chain, far_parts = [], [], [], [], [], []
    build = functools.partial(build_tiles, me, sb=sb, near=near, chips=chips)

    def target_job(emb):
        weights.append(target_operand(emb))
        return weights[-1]

    def near_job(chunks, back=None, planned=()):
        tile, table, rows, mass, *turned = build(
            [x for up, low, _ in chunks for x in (up, low)],
            weights,
            slots=slot_cap,
            offsets=tuple(offset for _, _, offset in chunks),
            chain=chain,
            back=back,
            planned=planned,
        )
        tiles.append(tile)
        tables.append(table)
        row_tiles.append(turned[0] if turned else tile)
        chain[:] = [rows, mass]
        return chain[0]

    def far_job():
        tile, at, sums, mass = build([to_group(far_both[0], 1)], weights[:1], slots=sb)
        far_parts.extend((tile, at, mass, to_group(sums, -1)))
        return sums

    jobs = [
        (0, lambda: target_job(in_hbm(target_emb)[0])),
        (0, lambda: target_job(sibling_emb)),
        (0, lambda: near_job([(upper, lower, 0)])),
    ]

    def behind_job(step, *halves):
        if jobs and jobs[0][0] <= max(0, step - 2):
            halves, _ = lax.optimization_barrier((halves, jobs.pop(0)[1]()))
        return halves

    up_a, up_b, down_a, down_b = upper, lower, upper, lower
    for step in range(1, steps + 1):
        if step > 1:
            up_a, down_b = behind_job(step, up_a, down_b)
        up_a, down_b = around(up_a, 1), around(down_b, -1)
        if step < steps:
            up_b, down_a = behind_job(step, up_b, down_a)
            up_b, down_a = around(up_b, 1), around(down_a, -1)
            chunks = [(up_a, up_b, -step), (down_a, down_b, step)]
            jobs.append((step, functools.partial(near_job, chunks)))
        if step == 1:
            far_both[0] = lax.optimization_barrier((both, up_a))[0]
    far_job()
    for _, job in jobs:
        job()
    far_tiles, far_at, far_mass, from_far = far_parts
    planned = plan_tiles(me, up_a, slot_cap, sb, target_emb.shape[0], near, chips, steps)
    near_job([(up_a, down_b, steps)], from_far, planned)
    near_rows, all_mass = chain

    for sweep in range(ITERS):
        if sweep > 0:
            back = to_group(extra, -1)
            near_rows = row_sums(tables, scale, across(scale, 1), row_tiles, chips * sb)
            near_rows = add_own(me, near_rows, back)
        bits = [1 << k for k in range(1, dev_count.bit_length() - 1)]
        parts = [near_rows]
        while bits:
            ways = [bits.pop() for _ in range(2 - len(bits) % 2)]
            ways = [sum(ways)] + ways if len(ways) == 2 else ways
            total = sum(parts[1:], parts[0])
            parts = [total] + [across(total, way) for way in ways]
        near_rows = add_all(parts)
        all_rows = to_group(near_rows, 1)
        mine, other = column_sums(tables, near_rows, all_mass, tiles, target_emb.shape[0])
        theirs = across(other, 1)
        own = (near_rows, source_mass) if sweep == ITERS - 1 else ()
        extra, scale = closing(
            me, far_at, all_rows, far_mass, mine, theirs, target_mass, far_tiles, *own
        )
    return (extra, scale)


def solution(mesh):
    placed = (
        P(("group", "dev"), None, None),
        P(("group", "dev"), None, None),
        P(("group", "dev"), None),
        P(("group", "dev"), None),
        P(("group", "dev"), None),
        P(("group", "dev"), None),
    )
    return jax.shard_map(
        local,
        mesh=mesh,
        in_specs=placed,
        out_specs=(P(("group", "dev"), None), P(("group", "dev"), None)),
        check_vma=False,
    )
```

```python
import functools
import math

import jax
import jax.numpy as jnp
from jax import lax
from jax.experimental import pallas as pl
from jax.experimental.pallas import tpu as pltpu
from jax.sharding import PartitionSpec as P

ITERS = 2

entropic_regularizer = 0.1
dustbin = 0.5
epsilon = 1e-06

VMEM = pl.BlockSpec(memory_space=pltpu.VMEM)
SMEM = pl.BlockSpec(memory_space=pltpu.SMEM)
HBM = pl.BlockSpec(memory_space=pltpu.HBM)
NT = (((1,), (1,)), ((), ()))
NN = (((1,), (0,)), ((), ()))


def in_vmem(*arrays):
    return [pltpu.with_memory_space_constraint(x, pltpu.VMEM) for x in arrays]


def in_smem(*arrays):
    return [pltpu.with_memory_space_constraint(x, pltpu.SMEM) for x in arrays]


def in_hbm(*arrays):
    return [pltpu.with_memory_space_constraint(x, pltpu.HBM) for x in arrays]


def split2(x):
    high = x.astype(jnp.bfloat16)
    low = (x - high.astype(jnp.float32)).astype(jnp.bfloat16)
    return high, low


def unit(x):
    return x * lax.rsqrt(jnp.mean(x * x, axis=-1, keepdims=True) + epsilon)


def stacked_parts(row):
    x = jnp.broadcast_to(row, (8, row.shape[1]))
    high = x.astype(jnp.bfloat16).astype(jnp.float32)
    rest = x - high
    low = rest.astype(jnp.bfloat16).astype(jnp.float32)
    place = lax.broadcasted_iota(jnp.int32, x.shape, 0)
    parts = jnp.where(place == 0, high, jnp.where(place == 1, low, jnp.where(place == 2, rest - low, 0.0)))
    return parts.astype(jnp.bfloat16)


def column_product(parts, tile):
    both = lax.dot_general(parts, tile, NN, preferred_element_type=jnp.float32)
    width = tile.shape[1] // 2
    return both[:, :width] + both[:, width:]


def row_product(parts, tile):
    return lax.dot_general(
        jnp.concatenate([parts, parts], axis=1), tile, NT, preferred_element_type=jnp.float32
    )


def target_kernel(emb_ref, out_ref, staged, arrived):
    parts = arrived.shape[0]
    share = emb_ref.shape[0] // parts
    copies = []
    for part in range(parts):
        spots = pl.ds(part * share, share)
        copies.append(pltpu.make_async_copy(emb_ref.at[spots], staged.at[spots], arrived.at[part]))
        copies[-1].start()

    def one(block, carry):
        high, low = split2(unit(staged[block]).T)
        out_ref[block] = jnp.concatenate([high, low], axis=1)
        return carry

    for part in range(parts):
        copies[part].wait()
        lax.fori_loop(part * share, (part + 1) * share, one, 0, unroll=4)


def target_operand(emb):
    blocks, rows, width = emb.shape
    parts = math.gcd(blocks, 8)
    return pl.pallas_call(
        target_kernel,
        out_shape=pltpu.VMEM((blocks, width, 2 * rows), jnp.bfloat16),
        in_specs=[pl.BlockSpec(memory_space=pl.ANY)],
        out_specs=VMEM,
        scratch_shapes=[pltpu.VMEM(emb.shape, jnp.float32), pltpu.SemaphoreType.DMA((parts,))],
        compiler_params=pltpu.CompilerParams(vmem_limit_bytes=16 << 20),
        name="target_operand",
    )(emb)


def pack_kernel(device, emb, mass, cand_device, cand_block, upper, lower, both, named, blocks, arrived):
    sb, rows, width = emb.shape
    half, near = rows // 2, cand_device.shape[1]
    copies = [
        pltpu.make_async_copy(cand_device, named, arrived.at[0]),
        pltpu.make_async_copy(cand_block, blocks, arrived.at[1]),
        pltpu.make_async_copy(mass, lower.at[pl.ds(sb * half, sb)], arrived.at[2]),
    ]
    for block in range(sb):
        into = pl.ds(block * half, half)
        copies.append(pltpu.make_async_copy(emb.at[block, pl.ds(0, half)], upper.at[into], arrived.at[3 + 2 * block]))
        copies.append(
            pltpu.make_async_copy(emb.at[block, pl.ds(half, half)], lower.at[into], arrived.at[4 + 2 * block])
        )
    for copy in copies:
        copy.start()
    for copy in copies[:2]:
        copy.wait()
    upper[sb * half :] = jnp.zeros((sb, width), jnp.float32)
    upper[sb * half :, 0:near] = named[...].astype(jnp.float32)
    upper[sb * half :, near : near + blocks.shape[1]] = blocks[...].astype(jnp.float32)
    for copy in copies[2:]:
        copy.wait()
    count = upper.shape[0]
    both[0:count] = upper[...]
    both[count:] = lower[...]


def pack(device, emb, mass, cand_device, cand_block):
    sb, rows, width = emb.shape
    count = sb * (rows // 2 + 1)
    shape = pltpu.VMEM((count, width), jnp.float32)
    return pl.pallas_call(
        pack_kernel,
        out_shape=(shape, shape, pltpu.VMEM((2 * count, width), jnp.float32)),
        in_specs=[SMEM] + [HBM] * 4,
        out_specs=(VMEM, VMEM, VMEM),
        scratch_shapes=[
            pltpu.VMEM(cand_device.shape, jnp.int32),
            pltpu.VMEM(cand_block.shape, jnp.int32),
            pltpu.SemaphoreType.DMA((3 + 2 * sb,)),
        ],
        compiler_params=pltpu.CompilerParams(vmem_limit_bytes=16 << 20),
        name="pack",
    )(device, *in_hbm(emb, mass, cand_device, cand_block))


def chip_at(chips, chip, offset):
    odd = lax.rem(chip, 2)
    spot = jnp.where(odd == 1, chips - 1 - chip // 2, chip // 2) + offset
    spot = jnp.where(spot < 0, spot + chips, jnp.where(spot >= chips, spot - chips, spot))
    return jnp.where(spot < chips // 2, 2 * spot, 2 * chips - 1 - 2 * spot)


def tile_kernel(plan, *refs):
    chunks, slots, sb, half, tb, near, offsets, far, chained, closing, planned = plan
    sides = 1 if far else 2
    refs = list(refs)
    device = refs.pop(0)
    if far:
        both = refs.pop(0)
        source = [both.at[pl.ds(start, sb * (half + 1))] for start in (0, sb * (half + 1))]
    else:
        source = [refs.pop(0) for _ in range(2 * chunks)]
    weight = [refs.pop(0) for _ in range(sides)]
    rows_in, mass_in = (refs.pop(0), refs.pop(0)) if chained else (None, None)
    back = refs.pop(0) if closing else None
    turned = None
    if planned:
        table, listed, tiles, rows_out, mass_out, partial, units = refs
    elif far:
        tiles, table, rows_out, mass_out, partial, units, staged, named, listed, arrived = refs
    else:
        tiles, table, rows_out, mass_out, turned, partial, units, staged, named, listed, arrived = refs
    count = chunks * sides * slots
    width = source[0].shape[1]
    scale = 1.0 / (width * entropic_regularizer)
    me = device[0]
    chips = rows_out.shape[0] // sb

    if not planned:
        copy = fetch_named([source[2 * chunk] for chunk in range(chunks)], staged, named, arrived, sb, half, me, near)
    if chained:
        rows_out[...] = rows_in[...]
        mass_out[...] = mass_in[...]
    partial[...] = jnp.zeros_like(partial)
    place = lax.broadcasted_iota(jnp.int32, (8, 2 * width), 0)
    ones = jnp.where(place == 0, 1.0, 0.0).astype(jnp.bfloat16)
    for chunk in range(chunks):
        for block in range(sb):
            rows = pl.ds(block * half, half)
            left = jnp.concatenate([source[2 * chunk][rows], source[2 * chunk + 1][rows]], axis=0)
            units[chunk * sb + block] = jnp.concatenate(split2(unit(left)), axis=1)
    chip_of = [jnp.int32(0) if far else chip_at(chips, me // 2, offsets[chunk]) for chunk in range(chunks)]
    if not planned:
        copy.wait()
        for chunk in range(chunks):
            if far:
                for j in range(sb):
                    listed[j] = j
                    table[j] = named[j, 2 * near]
            else:
                list_slots(named, listed, table, chip_of[chunk], chunk, slots, sb, tb, chips, count)

    for chunk in range(chunks):
        lower = source[2 * chunk + 1]
        for side in range(sides):
            for j in range(slots):
                at = (chunk * sides + side) * slots + j
                block = listed[at]
                right = weight[side][table[at] if far else lax.rem(table[count + at], tb)]
                both = lax.dot_general(
                    units[chunk * sb + lax.rem(block, sb)],
                    jnp.concatenate([right, right], axis=0),
                    NN,
                    preferred_element_type=jnp.float32,
                )
                nodes = both.shape[1] // 2
                affinity = both[:, :nodes] + both[:, nodes:]
                tile = jnp.exp(affinity * scale) * (1.0 / (8.0 * nodes))
                if turned is not None:
                    turned[at] = jnp.concatenate(split2(tile.T), axis=1)
                tile = jnp.concatenate(split2(tile), axis=1)
                tiles[at] = tile
                spot = chunk * (sb + 1) + block
                partial[spot] += lax.dot_general(ones, tile, NT, preferred_element_type=jnp.float32)
        start = pl.multiple_of(chip_of[chunk] * sb, sb)
        for block in range(sb):
            rows_out[pl.ds(start + block, 1)] = partial[chunk * (sb + 1) + block][0:1]
        mass_out[pl.ds(start, sb)] = lower[sb * half :]
    if closing:
        start = pl.multiple_of(me // 2 * sb, sb)
        rows_out[pl.ds(start, sb)] += back[...]


def fetch_named(uppers, staged, named, arrived, sb, half, me, near):
    for chunk, upper in enumerate(uppers):
        rows = upper[sb * half :]
        lane = lax.broadcasted_iota(jnp.int32, rows.shape, 1)
        blocks = pltpu.roll(rows, rows.shape[1] - near, 1)
        out = rows
        for side, wanted in enumerate((me, me + 1 - 2 * lax.rem(me, 2))):
            hit = jnp.where((rows.astype(jnp.int32) == wanted) & (lane < near), 1.0, 0.0)
            out = jnp.where(lane == 2 * side, jnp.sum(hit, axis=1, keepdims=True), out)
            out = jnp.where(lane == 2 * side + 1, jnp.sum(hit * blocks, axis=1, keepdims=True), out)
        staged[chunk * sb : (chunk + 1) * sb] = out.astype(jnp.int32)
    copy = pltpu.make_async_copy(staged, named, arrived)
    copy.start()
    return copy


def list_slots(named, listed, table, at_chip, chunk, slots, sb, tb, chips, count):
    for side in range(2):
        base = (chunk * 2 + side) * slots
        filled = jnp.int32(0)
        for block in range(sb):
            listed[base + filled] = block
            table[count + base + filled] = named[chunk * sb + block, 2 * side + 1]
            filled = filled + named[chunk * sb + block, 2 * side]
        for j in range(slots):
            valid = j < filled
            block = jnp.where(valid, listed[base + j], sb)
            which = jnp.where(valid, table[count + base + j], 2 * tb)
            listed[base + j] = block
            table[base + j] = jnp.where(valid, at_chip * sb + block, chips * sb)
            table[count + base + j] = jnp.where(valid, which + side * tb, 2 * tb)


def plan_kernel(plan, device, upper, table, listed, staged, named, arrived):
    slots, sb, half, tb, near, chips, offset = plan
    me = device[0]
    copy = fetch_named([upper], staged, named, arrived, sb, half, me, near)
    copy.wait()
    list_slots(named, listed, table, chip_at(chips, me // 2, offset), 0, slots, sb, tb, chips, 2 * slots)


def plan_tiles(device, upper, slots, sb, tb, near, chips, offset):
    half, width = upper.shape[0] // sb - 1, upper.shape[1]
    return pl.pallas_call(
        functools.partial(plan_kernel, (slots, sb, half, tb, near, chips, offset)),
        out_shape=(pltpu.SMEM((4 * slots + 1,), jnp.int32), pltpu.SMEM((2 * slots + 1,), jnp.int32)),
        in_specs=[SMEM, VMEM],
        out_specs=(SMEM, SMEM),
        scratch_shapes=[
            pltpu.VMEM((sb, width), jnp.int32),
            pltpu.SMEM((sb, width), jnp.int32),
            pltpu.SemaphoreType.DMA,
        ],
        compiler_params=SMALL,
        name="plan_tiles",
    )(device, upper)


def build_tiles(device, source, weight, slots, sb, near, chips, offsets=(), chain=(), back=None, planned=()):
    chunks, sides, far = max(1, len(source) // 2), len(weight), not offsets
    half, width = source[0].shape[0] // (sb * (1 + far)) - 1, source[0].shape[1]
    tb, nodes = weight[0].shape[0], weight[0].shape[2] // 2
    count = chunks * sides * slots
    plan = (
        *(chunks, slots, sb, half, tb, near, offsets, far),
        *(bool(chain), back is not None, bool(planned)),
    )
    operands = [*source, *in_vmem(*weight), *chain] + ([] if back is None else [back])
    rows = jax.ShapeDtypeStruct(((1 if far else chips) * sb, 2 * half), jnp.float32)
    out_shape = [
        pltpu.VMEM((count, 2 * half, 2 * nodes), jnp.bfloat16),
        pltpu.SMEM((count if far else 2 * count + 1,), jnp.int32),
        rows,
        rows,
    ]
    out_specs = [VMEM, SMEM, VMEM, VMEM]
    if not far and not planned:
        out_shape.append(pltpu.VMEM((count, nodes, 4 * half), jnp.bfloat16))
        out_specs.append(VMEM)
    scratch = [
        pltpu.VMEM((chunks * (sb + 1), 8, 2 * half), jnp.float32),
        pltpu.VMEM((chunks * sb, 2 * half, 2 * width), jnp.bfloat16),
        pltpu.VMEM((chunks * sb, width), jnp.int32),
        pltpu.SMEM((chunks * sb, width), jnp.int32),
        pltpu.SMEM((count + 1,), jnp.int32),
        pltpu.SemaphoreType.DMA,
    ]
    if planned:
        out_shape.pop(1)
        out_specs.pop(1)
        scratch = scratch[:2]
    out = pl.pallas_call(
        functools.partial(tile_kernel, plan),
        out_shape=out_shape,
        in_specs=[SMEM] + [VMEM] * len(operands) + [SMEM] * len(planned),
        out_specs=out_specs,
        scratch_shapes=scratch,
        compiler_params=pltpu.CompilerParams(vmem_limit_bytes=16 << 20),
        name="build_tiles",
    )(device, *operands, *in_smem(*planned))
    return [out[0], planned[0], *out[1:]] if planned else out


SMALL = pltpu.CompilerParams(vmem_limit_bytes=16 << 20)


def add_kernel(*refs):
    parts, total = refs[:-1], refs[-1]
    total[...] = sum([part[...] for part in parts[1:]], parts[0][...])


def add_all(parts):
    return pl.pallas_call(
        add_kernel,
        out_shape=jax.ShapeDtypeStruct(parts[0].shape, jnp.float32),
        in_specs=[VMEM] * len(parts),
        out_specs=VMEM,
        compiler_params=SMALL,
        name="add_all",
    )(*parts)


def insert_kernel(device, rows, part, out):
    out[...] = rows[...]
    out[pl.ds(pl.multiple_of(device[0] // 2 * part.shape[0], part.shape[0]), part.shape[0])] += part[...]


def add_own(device, rows, part):
    return pl.pallas_call(
        insert_kernel,
        out_shape=jax.ShapeDtypeStruct(rows.shape, jnp.float32),
        in_specs=[SMEM, VMEM, VMEM],
        out_specs=VMEM,
        compiler_params=SMALL,
        name="add_own",
    )(device, rows, part)


def column_kernel(counts, *refs):
    refs = list(refs)
    tables = [refs.pop(0) for _ in counts]
    rows, mass = refs.pop(0), refs.pop(0)
    tiles = [refs.pop(0) for _ in counts]
    own, other, scale, total = refs
    count, blocks = rows.shape[0], own.shape[0]
    scale[0:count] = mass[...] / (dustbin + rows[...])
    scale[count:] = jnp.zeros((8, scale.shape[1]), jnp.float32)
    total[...] = jnp.zeros_like(total)
    for part, slots in enumerate(counts):
        for slot in range(slots):
            parts = stacked_parts(scale[pl.ds(tables[part][slot], 1), :])
            total[tables[part][slots + slot]] += column_product(parts, tiles[part][slot])
    for block in range(blocks):
        own[block : block + 1] = jnp.sum(total[block], axis=0, keepdims=True)
        other[block : block + 1] = jnp.sum(total[blocks + block], axis=0, keepdims=True)


def column_sums(tables, rows, mass, tiles, targets):
    counts = tuple(t.shape[0] for t in tiles)
    width, nodes = rows.shape[1], tiles[0].shape[2] // 2
    return pl.pallas_call(
        functools.partial(column_kernel, counts),
        out_shape=(jax.ShapeDtypeStruct((targets, nodes), jnp.float32),) * 2,
        in_specs=[SMEM] * len(tables) + [VMEM] * (2 + len(tiles)),
        out_specs=(VMEM, VMEM),
        scratch_shapes=[
            pltpu.VMEM((rows.shape[0] + 8, width), jnp.float32),
            pltpu.VMEM((2 * targets + 1, 8, nodes), jnp.float32),
        ],
        compiler_params=SMALL,
        name="column_sums",
    )(*in_smem(*tables), rows, mass, *in_vmem(*tiles))


def closing_kernel(last, *refs):
    device, far_at, far_rows, far_mass, mine, theirs, target_mass, tiles = refs[:8]
    tgt, total = refs[-3], refs[-1]
    sb, slots = far_mass.shape[0], range(tiles.shape[0])
    start = pl.multiple_of(device[0] // 2 * sb, sb)
    scale = refs[-2]
    scale[...] = far_mass[...] / (dustbin + far_rows[pl.ds(start, sb)])
    total[...] = mine[...] + theirs[...]
    for slot in slots:
        product = column_product(stacked_parts(scale[slot : slot + 1, :]), tiles[slot])
        total[pl.ds(far_at[slot], 1)] += jnp.sum(product, axis=0, keepdims=True)
    tgt[...] = target_mass[...] / (dustbin + total[...])
    if last:
        rows, mass, src = refs[8:11]
        src[...] = mass[...] / (dustbin + rows[pl.ds(start, sb)])
    else:
        back = refs[8]
        for slot in slots:
            product = row_product(stacked_parts(tgt[pl.ds(far_at[slot], 1), :]), tiles[slot])
            back[slot : slot + 1] = jnp.sum(product, axis=0, keepdims=True)


def closing(device, far_at, far_rows, far_mass, mine, theirs, target_mass, tiles, rows=None, mass=None):
    last = mass is not None
    side = far_mass if mass is None else mass
    return pl.pallas_call(
        functools.partial(closing_kernel, last),
        out_shape=(
            jax.ShapeDtypeStruct(side.shape, jnp.float32),
            jax.ShapeDtypeStruct(target_mass.shape, jnp.float32),
        ),
        in_specs=[SMEM] * 2 + [VMEM] * (8 if last else 6),
        out_specs=(VMEM, VMEM),
        scratch_shapes=[pltpu.VMEM(far_mass.shape, jnp.float32), pltpu.VMEM(target_mass.shape, jnp.float32)],
        compiler_params=SMALL,
        name="closing",
    )(
        *(device, *in_smem(far_at), far_rows, far_mass, mine, theirs, target_mass, *in_vmem(tiles)),
        *((rows, mass) if last else ()),
    )


def row_kernel(counts, *refs):
    refs = list(refs)
    tables = [refs.pop(0) for _ in counts]
    mine, theirs = refs.pop(0), refs.pop(0)
    tiles = [refs.pop(0) for _ in counts]
    out, scale, total = refs
    blocks = mine.shape[0]
    scale[0:blocks] = mine[...]
    scale[blocks : 2 * blocks] = theirs[...]
    scale[2 * blocks :] = jnp.zeros((8, scale.shape[1]), jnp.float32)
    total[...] = jnp.zeros_like(total)
    for part, slots in enumerate(counts):
        for slot in range(slots):
            parts = stacked_parts(scale[pl.ds(tables[part][slots + slot], 1), :])
            product = row_product if part == len(counts) - 1 else column_product
            total[tables[part][slot]] += product(parts, tiles[part][slot])
    for block in range(out.shape[0]):
        out[block : block + 1] = jnp.sum(total[block], axis=0, keepdims=True)


def row_sums(tables, mine, theirs, tiles, sources):
    counts = tuple(t.shape[0] for t in tiles)
    width, nodes = tiles[0].shape[1], tiles[0].shape[2] // 2
    return pl.pallas_call(
        functools.partial(row_kernel, counts),
        out_shape=jax.ShapeDtypeStruct((sources, width), jnp.float32),
        in_specs=[SMEM] * len(tables) + [VMEM] * (2 + len(tiles)),
        out_specs=VMEM,
        scratch_shapes=[
            pltpu.VMEM((2 * mine.shape[0] + 8, nodes), jnp.float32),
            pltpu.VMEM((sources + 1, 8, width), jnp.float32),
        ],
        compiler_params=SMALL,
        name="row_sums",
    )(*in_smem(*tables), mine, theirs, *in_vmem(*tiles))


def local(source_emb, target_emb, source_mass, target_mass, cand_device, cand_block):
    dev_count = lax.axis_size("dev")
    group_count = lax.axis_size("group")
    chips = dev_count // 2
    sb, tb = source_emb.shape[0], target_emb.shape[0]
    near = cand_device.shape[1]
    slot_cap = (near * sb + dev_count - 1) // dev_count + 1
    steps = chips // 2
    ring = list(range(0, chips, 2)) + list(range(chips - 1, 0, -2))

    def around(x, by):
        pairs = [
            (2 * ring[i] + core, 2 * ring[(i + by) % chips] + core) for i in range(chips) for core in range(2)
        ]
        return lax.ppermute(x, "dev", pairs)

    def across(x, bit):
        return lax.ppermute(x, "dev", [(i, i ^ bit) for i in range(dev_count)])

    def to_group(x, by):
        return lax.ppermute(x, "group", [(g, (g + by) % group_count) for g in range(group_count)])

    device = lax.axis_index("dev").astype(jnp.int32)
    me = device.reshape(1)

    upper, lower, both = pack(me, source_emb, source_mass, cand_device, cand_block)
    sibling_emb = across(target_emb, 1)
    far_both = [both]

    weights, tiles, row_tiles, tables, chain, far_parts = [], [], [], [], [], []
    build = functools.partial(build_tiles, me, sb=sb, near=near, chips=chips)

    def target_job(emb):
        weights.append(target_operand(emb))
        return weights[-1]

    def near_job(chunks, back=None, planned=()):
        tile, table, rows, mass, *turned = build(
            [x for up, low, _ in chunks for x in (up, low)],
            weights,
            slots=slot_cap,
            offsets=tuple(offset for _, _, offset in chunks),
            chain=chain,
            back=back,
            planned=planned,
        )
        tiles.append(tile)
        tables.append(table)
        row_tiles.append(turned[0] if turned else tile)
        chain[:] = [rows, mass]
        return chain[0]

    def far_job():
        tile, at, sums, mass = build([to_group(far_both[0], 1)], weights[:1], slots=sb)
        far_parts.extend((tile, at, mass, to_group(sums, -1)))
        return sums

    jobs = [
        (0, lambda: target_job(in_hbm(target_emb)[0])),
        (0, lambda: target_job(sibling_emb)),
        (0, lambda: near_job([(upper, lower, 0)])),
    ]

    def behind_job(step, *halves):
        if jobs and jobs[0][0] <= max(0, step - 2):
            halves, _ = lax.optimization_barrier((halves, jobs.pop(0)[1]()))
        return halves

    up_a, up_b, down_a, down_b = upper, lower, upper, lower
    for step in range(1, steps + 1):
        if step > 1:
            up_a, down_b = behind_job(step, up_a, down_b)
        up_a, down_b = around(up_a, 1), around(down_b, -1)
        if step < steps:
            up_b, down_a = behind_job(step, up_b, down_a)
            up_b, down_a = around(up_b, 1), around(down_a, -1)
            chunks = [(up_a, up_b, -step), (down_a, down_b, step)]
            jobs.append((step, functools.partial(near_job, chunks)))
        if step == 1:
            far_both[0] = lax.optimization_barrier((both, up_a))[0]
    far_job()
    for _, job in jobs:
        job()
    far_tiles, far_at, far_mass, from_far = far_parts
    planned = plan_tiles(me, up_a, slot_cap, sb, target_emb.shape[0], near, chips, steps)
    near_job([(up_a, down_b, steps)], from_far, planned)
    near_rows, all_mass = chain

    for sweep in range(ITERS):
        if sweep > 0:
            back = to_group(extra, -1)
            near_rows = row_sums(tables, scale, across(scale, 1), row_tiles, chips * sb)
            near_rows = add_own(me, near_rows, back)
        bits = [1 << k for k in range(1, dev_count.bit_length() - 1)]
        parts = [near_rows]
        while bits:
            ways = [bits.pop() for _ in range(2 - len(bits) % 2)]
            ways = [sum(ways)] + ways if len(ways) == 2 else ways
            total = sum(parts[1:], parts[0])
            parts = [total] + [across(total, way) for way in ways]
        near_rows = add_all(parts)
        all_rows = to_group(near_rows, 1)
        mine, other = column_sums(tables, near_rows, all_mass, tiles, target_emb.shape[0])
        theirs = across(other, 1)
        own = (near_rows, source_mass) if sweep == ITERS - 1 else ()
        extra, scale = closing(
            me, far_at, all_rows, far_mass, mine, theirs, target_mass, far_tiles, *own
        )
    return (extra, scale)


def solution(mesh):
    placed = (
        P(("group", "dev"), None, None),
        P(("group", "dev"), None, None),
        P(("group", "dev"), None),
        P(("group", "dev"), None),
        P(("group", "dev"), None),
        P(("group", "dev"), None),
    )
    return jax.shard_map(
        local,
        mesh=mesh,
        in_specs=placed,
        out_specs=(P(("group", "dev"), None), P(("group", "dev"), None)),
        check_vma=False,
    )
```

```python
import functools
import math

import jax
import jax.numpy as jnp
from jax import lax
from jax.experimental import pallas as pl
from jax.experimental.pallas import tpu as pltpu
from jax.sharding import PartitionSpec as P

ITERS = 2

entropic_regularizer = 0.1
dustbin = 0.5
epsilon = 1e-06

VMEM = pl.BlockSpec(memory_space=pltpu.VMEM)
SMEM = pl.BlockSpec(memory_space=pltpu.SMEM)
HBM = pl.BlockSpec(memory_space=pltpu.HBM)
NT = (((1,), (1,)), ((), ()))
NN = (((1,), (0,)), ((), ()))


def in_vmem(*arrays):
    return [pltpu.with_memory_space_constraint(x, pltpu.VMEM) for x in arrays]


def in_smem(*arrays):
    return [pltpu.with_memory_space_constraint(x, pltpu.SMEM) for x in arrays]


def in_hbm(*arrays):
    return [pltpu.with_memory_space_constraint(x, pltpu.HBM) for x in arrays]


def split2(x):
    high = x.astype(jnp.bfloat16)
    low = (x - high.astype(jnp.float32)).astype(jnp.bfloat16)
    return high, low


def unit(x):
    return x * lax.rsqrt(jnp.mean(x * x, axis=-1, keepdims=True) + epsilon)


def stacked_parts(row):
    x = jnp.broadcast_to(row, (8, row.shape[1]))
    high = x.astype(jnp.bfloat16).astype(jnp.float32)
    rest = x - high
    low = rest.astype(jnp.bfloat16).astype(jnp.float32)
    place = lax.broadcasted_iota(jnp.int32, x.shape, 0)
    parts = jnp.where(place == 0, high, jnp.where(place == 1, low, jnp.where(place == 2, rest - low, 0.0)))
    return parts.astype(jnp.bfloat16)


def column_product(parts, tile):
    both = lax.dot_general(parts, tile, NN, preferred_element_type=jnp.float32)
    width = tile.shape[1] // 2
    return both[:, :width] + both[:, width:]


def row_product(parts, tile):
    return lax.dot_general(
        jnp.concatenate([parts, parts], axis=1), tile, NT, preferred_element_type=jnp.float32
    )


def target_kernel(emb_ref, out_ref, staged, arrived):
    parts = arrived.shape[0]
    share = emb_ref.shape[0] // parts
    copies = []
    for part in range(parts):
        spots = pl.ds(part * share, share)
        copies.append(pltpu.make_async_copy(emb_ref.at[spots], staged.at[spots], arrived.at[part]))
        copies[-1].start()

    def one(block, carry):
        high, low = split2(unit(staged[block]).T)
        out_ref[block] = jnp.concatenate([high, low], axis=1)
        return carry

    for part in range(parts):
        copies[part].wait()
        lax.fori_loop(part * share, (part + 1) * share, one, 0, unroll=4)


def target_operand(emb):
    blocks, rows, width = emb.shape
    parts = math.gcd(blocks, 8)
    return pl.pallas_call(
        target_kernel,
        out_shape=pltpu.VMEM((blocks, width, 2 * rows), jnp.bfloat16),
        in_specs=[pl.BlockSpec(memory_space=pl.ANY)],
        out_specs=VMEM,
        scratch_shapes=[pltpu.VMEM(emb.shape, jnp.float32), pltpu.SemaphoreType.DMA((parts,))],
        compiler_params=pltpu.CompilerParams(vmem_limit_bytes=16 << 20),
        name="target_operand",
    )(emb)


def pack_kernel(device, emb, mass, cand_device, cand_block, upper, lower, both, named, blocks, arrived):
    sb, rows, width = emb.shape
    half, near = rows // 2, cand_device.shape[1]
    copies = [
        pltpu.make_async_copy(cand_device, named, arrived.at[0]),
        pltpu.make_async_copy(cand_block, blocks, arrived.at[1]),
        pltpu.make_async_copy(mass, lower.at[pl.ds(sb * half, sb)], arrived.at[2]),
    ]
    for block in range(sb):
        into = pl.ds(block * half, half)
        copies.append(pltpu.make_async_copy(emb.at[block, pl.ds(0, half)], upper.at[into], arrived.at[3 + 2 * block]))
        copies.append(
            pltpu.make_async_copy(emb.at[block, pl.ds(half, half)], lower.at[into], arrived.at[4 + 2 * block])
        )
    for copy in copies:
        copy.start()
    for copy in copies[:2]:
        copy.wait()
    upper[sb * half :] = jnp.zeros((sb, width), jnp.float32)
    upper[sb * half :, 0:near] = named[...].astype(jnp.float32)
    upper[sb * half :, near : near + blocks.shape[1]] = blocks[...].astype(jnp.float32)
    for copy in copies[2:]:
        copy.wait()
    count = upper.shape[0]
    both[0:count] = upper[...]
    both[count:] = lower[...]


def pack(device, emb, mass, cand_device, cand_block):
    sb, rows, width = emb.shape
    count = sb * (rows // 2 + 1)
    shape = pltpu.VMEM((count, width), jnp.float32)
    return pl.pallas_call(
        pack_kernel,
        out_shape=(shape, shape, pltpu.VMEM((2 * count, width), jnp.float32)),
        in_specs=[SMEM] + [HBM] * 4,
        out_specs=(VMEM, VMEM, VMEM),
        scratch_shapes=[
            pltpu.VMEM(cand_device.shape, jnp.int32),
            pltpu.VMEM(cand_block.shape, jnp.int32),
            pltpu.SemaphoreType.DMA((3 + 2 * sb,)),
        ],
        compiler_params=pltpu.CompilerParams(vmem_limit_bytes=16 << 20),
        name="pack",
    )(device, *in_hbm(emb, mass, cand_device, cand_block))


def chip_at(chips, chip, offset):
    odd = lax.rem(chip, 2)
    spot = jnp.where(odd == 1, chips - 1 - chip // 2, chip // 2) + offset
    spot = jnp.where(spot < 0, spot + chips, jnp.where(spot >= chips, spot - chips, spot))
    return jnp.where(spot < chips // 2, 2 * spot, 2 * chips - 1 - 2 * spot)


def tile_kernel(plan, *refs):
    chunks, slots, sb, half, tb, near, offsets, far, chained, closing, planned = plan
    sides = 1 if far else 2
    refs = list(refs)
    device = refs.pop(0)
    if far:
        both = refs.pop(0)
        source = [both.at[pl.ds(start, sb * (half + 1))] for start in (0, sb * (half + 1))]
    else:
        source = [refs.pop(0) for _ in range(2 * chunks)]
    weight = [refs.pop(0) for _ in range(sides)]
    rows_in, mass_in = (refs.pop(0), refs.pop(0)) if chained else (None, None)
    back = refs.pop(0) if closing else None
    turned = None
    if planned:
        table, listed, tiles, rows_out, mass_out, partial, units = refs
    elif far:
        tiles, table, rows_out, mass_out, partial, units, staged, named, listed, arrived = refs
    else:
        tiles, table, rows_out, mass_out, turned, partial, units, staged, named, listed, arrived = refs
    count = chunks * sides * slots
    width = source[0].shape[1]
    scale = 1.0 / (width * entropic_regularizer)
    me = device[0]
    chips = rows_out.shape[0] // sb

    if not planned:
        copy = fetch_named([source[2 * chunk] for chunk in range(chunks)], staged, named, arrived, sb, half, me, near)
    if chained:
        rows_out[...] = rows_in[...]
        mass_out[...] = mass_in[...]
    partial[...] = jnp.zeros_like(partial)
    place = lax.broadcasted_iota(jnp.int32, (8, 2 * width), 0)
    ones = jnp.where(place == 0, 1.0, 0.0).astype(jnp.bfloat16)
    for chunk in range(chunks):
        for block in range(sb):
            rows = pl.ds(block * half, half)
            left = jnp.concatenate([source[2 * chunk][rows], source[2 * chunk + 1][rows]], axis=0)
            units[chunk * sb + block] = jnp.concatenate(split2(unit(left)), axis=1)
    chip_of = [jnp.int32(0) if far else chip_at(chips, me // 2, offsets[chunk]) for chunk in range(chunks)]
    if not planned:
        copy.wait()
        for chunk in range(chunks):
            if far:
                for j in range(sb):
                    listed[j] = j
                    table[j] = named[j, 2 * near]
            else:
                list_slots(named, listed, table, chip_of[chunk], chunk, slots, sb, tb, chips, count)

    for chunk in range(chunks):
        lower = source[2 * chunk + 1]
        for side in range(sides):
            for j in range(slots):
                at = (chunk * sides + side) * slots + j
                block = listed[at]
                right = weight[side][table[at] if far else lax.rem(table[count + at], tb)]
                both = lax.dot_general(
                    units[chunk * sb + lax.rem(block, sb)],
                    jnp.concatenate([right, right], axis=0),
                    NN,
                    preferred_element_type=jnp.float32,
                )
                nodes = both.shape[1] // 2
                affinity = both[:, :nodes] + both[:, nodes:]
                tile = jnp.exp(affinity * scale) * (1.0 / (8.0 * nodes))
                if turned is not None:
                    turned[at] = jnp.concatenate(split2(tile.T), axis=1)
                tile = jnp.concatenate(split2(tile), axis=1)
                tiles[at] = tile
                spot = chunk * (sb + 1) + block
                partial[spot] += lax.dot_general(ones, tile, NT, preferred_element_type=jnp.float32)
        start = pl.multiple_of(chip_of[chunk] * sb, sb)
        for block in range(sb):
            rows_out[pl.ds(start + block, 1)] = partial[chunk * (sb + 1) + block][0:1]
        mass_out[pl.ds(start, sb)] = lower[sb * half :]
    if closing:
        start = pl.multiple_of(me // 2 * sb, sb)
        rows_out[pl.ds(start, sb)] += back[...]


def fetch_named(uppers, staged, named, arrived, sb, half, me, near):
    for chunk, upper in enumerate(uppers):
        rows = upper[sb * half :]
        lane = lax.broadcasted_iota(jnp.int32, rows.shape, 1)
        blocks = pltpu.roll(rows, rows.shape[1] - near, 1)
        out = rows
        for side, wanted in enumerate((me, me + 1 - 2 * lax.rem(me, 2))):
            hit = jnp.where((rows.astype(jnp.int32) == wanted) & (lane < near), 1.0, 0.0)
            out = jnp.where(lane == 2 * side, jnp.sum(hit, axis=1, keepdims=True), out)
            out = jnp.where(lane == 2 * side + 1, jnp.sum(hit * blocks, axis=1, keepdims=True), out)
        staged[chunk * sb : (chunk + 1) * sb] = out.astype(jnp.int32)
    copy = pltpu.make_async_copy(staged, named, arrived)
    copy.start()
    return copy


def list_slots(named, listed, table, at_chip, chunk, slots, sb, tb, chips, count):
    for side in range(2):
        base = (chunk * 2 + side) * slots
        filled = jnp.int32(0)
        for block in range(sb):
            listed[base + filled] = block
            table[count + base + filled] = named[chunk * sb + block, 2 * side + 1]
            filled = filled + named[chunk * sb + block, 2 * side]
        for j in range(slots):
            valid = j < filled
            block = jnp.where(valid, listed[base + j], sb)
            which = jnp.where(valid, table[count + base + j], 2 * tb)
            listed[base + j] = block
            table[base + j] = jnp.where(valid, at_chip * sb + block, chips * sb)
            table[count + base + j] = jnp.where(valid, which + side * tb, 2 * tb)


def plan_kernel(plan, device, upper, table, listed, staged, named, arrived):
    slots, sb, half, tb, near, chips, offset = plan
    me = device[0]
    copy = fetch_named([upper], staged, named, arrived, sb, half, me, near)
    copy.wait()
    list_slots(named, listed, table, chip_at(chips, me // 2, offset), 0, slots, sb, tb, chips, 2 * slots)


def plan_tiles(device, upper, slots, sb, tb, near, chips, offset):
    half, width = upper.shape[0] // sb - 1, upper.shape[1]
    return pl.pallas_call(
        functools.partial(plan_kernel, (slots, sb, half, tb, near, chips, offset)),
        out_shape=(pltpu.SMEM((4 * slots + 1,), jnp.int32), pltpu.SMEM((2 * slots + 1,), jnp.int32)),
        in_specs=[SMEM, VMEM],
        out_specs=(SMEM, SMEM),
        scratch_shapes=[
            pltpu.VMEM((sb, width), jnp.int32),
            pltpu.SMEM((sb, width), jnp.int32),
            pltpu.SemaphoreType.DMA,
        ],
        compiler_params=SMALL,
        name="plan_tiles",
    )(device, upper)


def build_tiles(device, source, weight, slots, sb, near, chips, offsets=(), chain=(), back=None, planned=()):
    chunks, sides, far = max(1, len(source) // 2), len(weight), not offsets
    half, width = source[0].shape[0] // (sb * (1 + far)) - 1, source[0].shape[1]
    tb, nodes = weight[0].shape[0], weight[0].shape[2] // 2
    count = chunks * sides * slots
    plan = (
        *(chunks, slots, sb, half, tb, near, offsets, far),
        *(bool(chain), back is not None, bool(planned)),
    )
    operands = [*source, *in_vmem(*weight), *chain] + ([] if back is None else [back])
    rows = jax.ShapeDtypeStruct(((1 if far else chips) * sb, 2 * half), jnp.float32)
    out_shape = [
        pltpu.VMEM((count, 2 * half, 2 * nodes), jnp.bfloat16),
        pltpu.SMEM((count if far else 2 * count + 1,), jnp.int32),
        rows,
        rows,
    ]
    out_specs = [VMEM, SMEM, VMEM, VMEM]
    if not far and not planned:
        out_shape.append(pltpu.VMEM((count, nodes, 4 * half), jnp.bfloat16))
        out_specs.append(VMEM)
    scratch = [
        pltpu.VMEM((chunks * (sb + 1), 8, 2 * half), jnp.float32),
        pltpu.VMEM((chunks * sb, 2 * half, 2 * width), jnp.bfloat16),
        pltpu.VMEM((chunks * sb, width), jnp.int32),
        pltpu.SMEM((chunks * sb, width), jnp.int32),
        pltpu.SMEM((count + 1,), jnp.int32),
        pltpu.SemaphoreType.DMA,
    ]
    if planned:
        out_shape.pop(1)
        out_specs.pop(1)
        scratch = scratch[:2]
    out = pl.pallas_call(
        functools.partial(tile_kernel, plan),
        out_shape=out_shape,
        in_specs=[SMEM] + [VMEM] * len(operands) + [SMEM] * len(planned),
        out_specs=out_specs,
        scratch_shapes=scratch,
        compiler_params=pltpu.CompilerParams(vmem_limit_bytes=16 << 20),
        name="build_tiles",
    )(device, *operands, *in_smem(*planned))
    return [out[0], planned[0], *out[1:]] if planned else out


SMALL = pltpu.CompilerParams(vmem_limit_bytes=16 << 20)


def add_kernel(*refs):
    parts, total = refs[:-1], refs[-1]
    total[...] = sum([part[...] for part in parts[1:]], parts[0][...])


def add_all(parts):
    return pl.pallas_call(
        add_kernel,
        out_shape=jax.ShapeDtypeStruct(parts[0].shape, jnp.float32),
        in_specs=[VMEM] * len(parts),
        out_specs=VMEM,
        compiler_params=SMALL,
        name="add_all",
    )(*parts)


def insert_kernel(device, rows, part, out):
    out[...] = rows[...]
    out[pl.ds(pl.multiple_of(device[0] // 2 * part.shape[0], part.shape[0]), part.shape[0])] += part[...]


def add_own(device, rows, part):
    return pl.pallas_call(
        insert_kernel,
        out_shape=jax.ShapeDtypeStruct(rows.shape, jnp.float32),
        in_specs=[SMEM, VMEM, VMEM],
        out_specs=VMEM,
        compiler_params=SMALL,
        name="add_own",
    )(device, rows, part)


def column_kernel(counts, *refs):
    refs = list(refs)
    tables = [refs.pop(0) for _ in counts]
    rows, mass = refs.pop(0), refs.pop(0)
    tiles = [refs.pop(0) for _ in counts]
    own, other, scale, total = refs
    count, blocks = rows.shape[0], own.shape[0]
    scale[0:count] = mass[...] / (dustbin + rows[...])
    scale[count:] = jnp.zeros((8, scale.shape[1]), jnp.float32)
    total[...] = jnp.zeros_like(total)
    for part, slots in enumerate(counts):
        for slot in range(slots):
            parts = stacked_parts(scale[pl.ds(tables[part][slot], 1), :])
            total[tables[part][slots + slot]] += column_product(parts, tiles[part][slot])
    for block in range(blocks):
        own[block : block + 1] = jnp.sum(total[block], axis=0, keepdims=True)
        other[block : block + 1] = jnp.sum(total[blocks + block], axis=0, keepdims=True)


def column_sums(tables, rows, mass, tiles, targets):
    counts = tuple(t.shape[0] for t in tiles)
    width, nodes = rows.shape[1], tiles[0].shape[2] // 2
    return pl.pallas_call(
        functools.partial(column_kernel, counts),
        out_shape=(jax.ShapeDtypeStruct((targets, nodes), jnp.float32),) * 2,
        in_specs=[SMEM] * len(tables) + [VMEM] * (2 + len(tiles)),
        out_specs=(VMEM, VMEM),
        scratch_shapes=[
            pltpu.VMEM((rows.shape[0] + 8, width), jnp.float32),
            pltpu.VMEM((2 * targets + 1, 8, nodes), jnp.float32),
        ],
        compiler_params=SMALL,
        name="column_sums",
    )(*in_smem(*tables), rows, mass, *in_vmem(*tiles))


def closing_kernel(last, *refs):
    device, far_at, far_rows, far_mass, mine, theirs, target_mass, tiles = refs[:8]
    tgt, total = refs[-3], refs[-1]
    sb, slots = far_mass.shape[0], range(tiles.shape[0])
    start = pl.multiple_of(device[0] // 2 * sb, sb)
    scale = refs[-2]
    scale[...] = far_mass[...] / (dustbin + far_rows[pl.ds(start, sb)])
    total[...] = mine[...] + theirs[...]
    for slot in slots:
        product = column_product(stacked_parts(scale[slot : slot + 1, :]), tiles[slot])
        total[pl.ds(far_at[slot], 1)] += jnp.sum(product, axis=0, keepdims=True)
    tgt[...] = target_mass[...] / (dustbin + total[...])
    if last:
        rows, mass, src = refs[8:11]
        src[...] = mass[...] / (dustbin + rows[pl.ds(start, sb)])
    else:
        back = refs[8]
        for slot in slots:
            product = row_product(stacked_parts(tgt[pl.ds(far_at[slot], 1), :]), tiles[slot])
            back[slot : slot + 1] = jnp.sum(product, axis=0, keepdims=True)


def closing(device, far_at, far_rows, far_mass, mine, theirs, target_mass, tiles, rows=None, mass=None):
    last = mass is not None
    side = far_mass if mass is None else mass
    return pl.pallas_call(
        functools.partial(closing_kernel, last),
        out_shape=(
            jax.ShapeDtypeStruct(side.shape, jnp.float32),
            jax.ShapeDtypeStruct(target_mass.shape, jnp.float32),
        ),
        in_specs=[SMEM] * 2 + [VMEM] * (8 if last else 6),
        out_specs=(VMEM, VMEM),
        scratch_shapes=[pltpu.VMEM(far_mass.shape, jnp.float32), pltpu.VMEM(target_mass.shape, jnp.float32)],
        compiler_params=SMALL,
        name="closing",
    )(
        *(device, *in_smem(far_at), far_rows, far_mass, mine, theirs, target_mass, *in_vmem(tiles)),
        *((rows, mass) if last else ()),
    )


def row_kernel(counts, *refs):
    refs = list(refs)
    tables = [refs.pop(0) for _ in counts]
    mine, theirs = refs.pop(0), refs.pop(0)
    tiles = [refs.pop(0) for _ in counts]
    out, scale, total = refs
    blocks = mine.shape[0]
    scale[0:blocks] = mine[...]
    scale[blocks : 2 * blocks] = theirs[...]
    scale[2 * blocks :] = jnp.zeros((8, scale.shape[1]), jnp.float32)
    total[...] = jnp.zeros_like(total)
    for part, slots in enumerate(counts):
        for slot in range(slots):
            parts = stacked_parts(scale[pl.ds(tables[part][slots + slot], 1), :])
            product = row_product if part == len(counts) - 1 else column_product
            total[tables[part][slot]] += product(parts, tiles[part][slot])
    for block in range(out.shape[0]):
        out[block : block + 1] = jnp.sum(total[block], axis=0, keepdims=True)


def row_sums(tables, mine, theirs, tiles, sources):
    counts = tuple(t.shape[0] for t in tiles)
    width, nodes = tiles[0].shape[1], tiles[0].shape[2] // 2
    return pl.pallas_call(
        functools.partial(row_kernel, counts),
        out_shape=jax.ShapeDtypeStruct((sources, width), jnp.float32),
        in_specs=[SMEM] * len(tables) + [VMEM] * (2 + len(tiles)),
        out_specs=VMEM,
        scratch_shapes=[
            pltpu.VMEM((2 * mine.shape[0] + 8, nodes), jnp.float32),
            pltpu.VMEM((sources + 1, 8, width), jnp.float32),
        ],
        compiler_params=SMALL,
        name="row_sums",
    )(*in_smem(*tables), mine, theirs, *in_vmem(*tiles))


def local(source_emb, target_emb, source_mass, target_mass, cand_device, cand_block):
    dev_count = lax.axis_size("dev")
    group_count = lax.axis_size("group")
    chips = dev_count // 2
    sb, tb = source_emb.shape[0], target_emb.shape[0]
    near = cand_device.shape[1]
    slot_cap = (near * sb + dev_count - 1) // dev_count + 1
    steps = chips // 2
    ring = list(range(0, chips, 2)) + list(range(chips - 1, 0, -2))

    def around(x, by):
        pairs = [
            (2 * ring[i] + core, 2 * ring[(i + by) % chips] + core) for i in range(chips) for core in range(2)
        ]
        return lax.ppermute(x, "dev", pairs)

    def across(x, bit):
        return lax.ppermute(x, "dev", [(i, i ^ bit) for i in range(dev_count)])

    def to_group(x, by):
        return lax.ppermute(x, "group", [(g, (g + by) % group_count) for g in range(group_count)])

    device = lax.axis_index("dev").astype(jnp.int32)
    me = device.reshape(1)

    upper, lower, both = pack(me, source_emb, source_mass, cand_device, cand_block)
    sibling_emb = across(target_emb, 1)
    far_both = [both]

    weights, tiles, row_tiles, tables, chain, far_parts = [], [], [], [], [], []
    build = functools.partial(build_tiles, me, sb=sb, near=near, chips=chips)

    def target_job(emb):
        weights.append(target_operand(emb))
        return weights[-1]

    def near_job(chunks, back=None, planned=()):
        tile, table, rows, mass, *turned = build(
            [x for up, low, _ in chunks for x in (up, low)],
            weights,
            slots=slot_cap,
            offsets=tuple(offset for _, _, offset in chunks),
            chain=chain,
            back=back,
            planned=planned,
        )
        tiles.append(tile)
        tables.append(table)
        row_tiles.append(turned[0] if turned else tile)
        chain[:] = [rows, mass]
        return chain[0]

    def far_job():
        tile, at, sums, mass = build([to_group(far_both[0], 1)], weights[:1], slots=sb)
        far_parts.extend((tile, at, mass, to_group(sums, -1)))
        return sums

    jobs = [
        (0, lambda: target_job(in_hbm(target_emb)[0])),
        (0, lambda: target_job(sibling_emb)),
        (0, lambda: near_job([(upper, lower, 0)])),
        (0, None),
    ]

    def behind_job(step, *halves):
        if jobs and jobs[0][0] <= max(0, step - 2):
            job = jobs.pop(0)[1]
            if job is not None:
                halves, _ = lax.optimization_barrier((halves, job()))
        return halves

    up_a, up_b, down_a, down_b = upper, lower, upper, lower
    for step in range(1, steps + 1):
        if step > 1:
            up_a, down_b = behind_job(step, up_a, down_b)
        up_a, down_b = around(up_a, 1), around(down_b, -1)
        if step < steps:
            up_b, down_a = behind_job(step, up_b, down_a)
            up_b, down_a = around(up_b, 1), around(down_a, -1)
            chunks = [(up_a, up_b, -step), (down_a, down_b, step)]
            jobs.append((step, functools.partial(near_job, chunks)))
        if step == 1:
            far_both[0] = lax.optimization_barrier((both, up_a))[0]
    far_job()
    for _, job in jobs:
        job()
    far_tiles, far_at, far_mass, from_far = far_parts
    planned = plan_tiles(me, up_a, slot_cap, sb, target_emb.shape[0], near, chips, steps)
    near_job([(up_a, down_b, steps)], from_far, planned)
    near_rows, all_mass = chain

    for sweep in range(ITERS):
        if sweep > 0:
            back = to_group(extra, -1)
            near_rows = row_sums(tables, scale, across(scale, 1), row_tiles, chips * sb)
            near_rows = add_own(me, near_rows, back)
        bits = [1 << k for k in range(1, dev_count.bit_length() - 1)]
        parts = [near_rows]
        while bits:
            ways = [bits.pop() for _ in range(2 - len(bits) % 2)]
            ways = [sum(ways)] + ways if len(ways) == 2 else ways
            total = sum(parts[1:], parts[0])
            parts = [total] + [across(total, way) for way in ways]
        near_rows = add_all(parts)
        all_rows = to_group(near_rows, 1)
        mine, other = column_sums(tables, near_rows, all_mass, tiles, target_emb.shape[0])
        theirs = across(other, 1)
        own = (near_rows, source_mass) if sweep == ITERS - 1 else ()
        extra, scale = closing(
            me, far_at, all_rows, far_mass, mine, theirs, target_mass, far_tiles, *own
        )
    return (extra, scale)


def solution(mesh):
    placed = (
        P(("group", "dev"), None, None),
        P(("group", "dev"), None, None),
        P(("group", "dev"), None),
        P(("group", "dev"), None),
        P(("group", "dev"), None),
        P(("group", "dev"), None),
    )
    return jax.shard_map(
        local,
        mesh=mesh,
        in_specs=placed,
        out_specs=(P(("group", "dev"), None), P(("group", "dev"), None)),
        check_vma=False,
    )
```
